128 devices in a mesh: tensor: 4 (over y), context: 4 (over x_hi, core), dp: 8 (over z, x_lo).
Axes of the slice: x: 4 (x_hi: 2, x_lo: 2; x = x_hi * 2 + x_lo), y: 4, z: 4, core: 2. Of those that a mesh axis runs over, the one named last changes fastest.
Arguments:
- tokens: bfloat16 [16384, 4096], P(('tensor', 'context', 'dp')), may hold values from -6 to 6
- gates: float32 [16384, 2], P(('tensor', 'context', 'dp')), may hold values from 0.1 to 0.9
- routes: int32 [16384, 2], P(('tensor', 'context', 'dp')), may hold values from 0 to 15, all different within a row; in each aligned block of 128 rows (0 to 127, 128 to 255, ...) at most 24 rows name the same one
- w_in: bfloat16 [16, 4096, 1536], P(('tensor', 'context')), may hold values from -0.09375 to 0.09375
- w_out: bfloat16 [16, 768, 4096], P(('tensor', 'context')), may hold values from -0.21875 to 0.21875
- cotangent: bfloat16 [16384, 4096], P(('tensor', 'context', 'dp')), may hold values from -6 to 6
Outputs:
- mixed: bfloat16 [16384, 4096], P(('tensor', 'context', 'dp'))
- grad_tokens: bfloat16 [16384, 4096], P(('tensor', 'context', 'dp'))
- grad_gates: float32 [16384, 2], P(('tensor', 'context', 'dp'))
- grad_w_in: bfloat16 [65536, 1536], P(('tensor', 'context', 'dp'))
- grad_w_out: bfloat16 [12288, 4096], P(('tensor', 'context', 'dp'))
The draws below stay inside these ranges and needn't reach their ends.
Inputs may be any that keep to these rules, and one draw needn't show every extreme that they name: `routes`: each row names 2 different experts; among the 128 rows of one device (aligned blocks) no expert is named more than 24 times, a bound that some block reaches.
All inputs are finite; a program needn't handle non-finite values.
Results may differ from the reference program's by a relative error of at most 0.019.
Values may be sent and summed in bfloat16 or wider, within the bound.
A program may use at most 128 MiB of HBM per device.

```python
import math
import jax
import jax.numpy as jnp
import numpy as np
from jax import lax

D = 4096
F = 768
TOP = 2
TOK_DEV = 128
EXPERTS = 16
REPLICAS = 8
MOST = 24
TOKENS = 16384


def block_scale(own_key, extent, pieces, smallest, high):
    def one(position, blocks):
        steps = jax.random.uniform(jax.random.fold_in(jax.random.fold_in(own_key, 6), position), (blocks,), jnp.float32, smallest / len(pieces), high / len(pieces))
        return jnp.repeat(jnp.exp(steps), extent[position] // blocks).reshape((-1,) + (1,) * (len(extent) - position - 1))

    factor_of = one(*pieces[0])
    for cut in pieces[1:]:
        factor_of = factor_of * one(*cut)
    return factor_of


def assign_block(own_key, own, number, rows, number_of, top, limit, lean):
    order = jax.random.permutation(own_key, number_of)
    crowded, usual = load_shares(number_of, rows * top, limit, lean, True), load_shares(number_of, rows * top, limit, lean, False)
    places = jnp.arange(number_of)

    def named(tallies, rotation):
        used = int((tallies > 0).sum())
        fixed = max(1, used // 4)
        moved = fixed + (places - fixed + rotation * (used - fixed)) % max(1, number_of - fixed)
        return jnp.zeros((number_of,), jnp.int32).at[order[jnp.where(places < fixed, places, moved)]].set(jnp.asarray(tallies, jnp.int32))

    tallies = jnp.where(number % 4 == 0, named(crowded, number // 4), named(usual, number - number // 4 - 1))
    mixed = jax.random.permutation(jax.random.fold_in(own, 3), number_of)
    giver, sink = mixed[0:number_of // 2 * 2:2], mixed[1:number_of // 2 * 2:2]
    margin = jnp.minimum(tallies[giver] - 1, limit - tallies[sink]) // 2
    margin = jnp.where((giver == order[0]) | (sink == order[0]) | (tallies[sink] == 0), 0, jnp.maximum(margin, 0))
    moved = jax.random.randint(jax.random.fold_in(own, 4), (number_of // 2,), 0, 1 << 20) % (margin + 1)
    tallies = tallies.at[giver].add(-moved).at[sink].add(moved)
    members = jnp.searchsorted(jnp.cumsum(tallies), jnp.arange(rows * top), side="right").astype(jnp.int32)
    table = members.reshape(top, rows).T
    table = table[jax.random.permutation(jax.random.fold_in(own, 1), rows)]
    rotation = jax.random.randint(jax.random.fold_in(own, 2), (rows, 1), 0, top)
    return jnp.take_along_axis(table, (jnp.arange(top)[None, :] + rotation) % top, axis=1)


def load_shares(count, total, reach, skew, full):
    portions = [(1 << 20) // math.isqrt(rank ** skew) + 1 for rank in range(1, count + 1)]
    largest = reach if full else min(reach, max(-(-total // count), total * portions[0] // sum(portions)))
    least = 1 if total - largest >= count - 1 else 0
    given, spare = [largest] + [least] * (count - 1), total - largest - least * (count - 1)
    while spare > 0:
        movable = [i for i in range(1, count) if given[i] < largest] or [i for i in range(1, count) if given[i] < reach]
        pool, budget = sum([portions[i] for i in movable]), spare
        for i in movable:
            addition = min(reach - given[i], max(1, budget * portions[i] // pool), spare)
            given[i] = given[i] + addition
            spare = spare - addition
    return np.array(given)


def normal_values(own_key, extent, scale, limit, cuts=(), kind=jnp.bfloat16):
    values = jax.random.normal(own_key, extent, jnp.float32) * scale
    if len(cuts) > 0:
        values = block_scale(own_key, extent, cuts, -0.22, 0.18) * values
    return jnp.clip(values, min=-limit, max=limit).astype(kind)


def setup_inputs(seed: int = 0) -> dict:
    keys = jax.random.split(jax.random.key(seed), 7)
    tokens = normal_values(keys[0], (TOKENS, D), 1.0, 6.0, ((0, 128),))
    gates = jnp.clip(0.1 + 0.79999997 * jax.random.uniform(keys[1], (TOKENS, TOP), jnp.float32) ** block_scale(keys[1], (TOKENS, TOP), ((0, 128),), -0.2, 0.2), 0.1, 0.9)
    routes_keys = jax.random.split(jax.random.fold_in(keys[2], 1), TOKENS // TOK_DEV)
    routes_turns = jax.random.permutation(jax.random.fold_in(keys[2], 3), TOKENS // TOK_DEV)
    routes = jax.vmap(lambda own, number: assign_block(jax.random.fold_in(keys[2], 2), own, number, TOK_DEV, EXPERTS, TOP, MOST, 2))(routes_keys, routes_turns).reshape((TOKENS, TOP))
    w_in = normal_values(keys[3], (EXPERTS, D, 2 * F), D ** -0.5, 0.09375, ((0, 16),))
    w_out = normal_values(keys[4], (EXPERTS, F, D), F ** -0.5, 0.21875, ((0, 16),))
    cotangent = normal_values(keys[5], (TOKENS, D), 1.0, 6.0, ((0, 128),))
    return {"tokens": tokens, "gates": gates, "routes": routes, "w_in": w_in, "w_out": w_out, "cotangent": cotangent}


def block_tables(route_ids):
    total_routes = TOK_DEV * TOP
    matches = (route_ids[:, None] == jnp.arange(EXPERTS, dtype=jnp.int32)[None, :]).astype(jnp.int32)
    slot_index = jnp.sum((jnp.cumsum(matches, axis=0) - matches) * matches, axis=1)
    positions = route_ids * MOST + slot_index
    empty = jnp.full((EXPERTS * MOST,), total_routes, jnp.int32)
    slot_table = empty.at[positions].set(jnp.arange(total_routes, dtype=jnp.int32))
    return slot_table.reshape(EXPERTS, MOST), positions


def reference(tokens, gates, routes, w_in, w_out, cotangent):
    blocks = TOKENS // TOK_DEV
    total_routes = TOK_DEV * TOP
    tables, positions = jax.vmap(block_tables)(routes.reshape(blocks, total_routes))
    block_base = jnp.arange(blocks, dtype=jnp.int32)[:, None]
    flat_gates = gates.reshape(-1)

    def expert_pass(expert):
        slot_table = tables[:, expert, :]
        occupied = (slot_table < total_routes).reshape(-1)
        safe_routes = jnp.minimum(slot_table, total_routes - 1)
        token_rows = (block_base * TOK_DEV + safe_routes // TOP).reshape(-1)
        route_rows = (block_base * total_routes + safe_routes).reshape(-1)
        inputs_here = jnp.where(occupied[:, None], tokens[token_rows], jnp.zeros((), tokens.dtype))
        route_gate = jnp.where(occupied, flat_gates[route_rows], jnp.zeros((), flat_gates.dtype))
        grads_here = (route_gate[:, None] * cotangent[token_rows].astype(jnp.float32)).astype(jnp.bfloat16)
        weight_in = w_in[expert]
        weight_out = w_out[expert]
        gate_up = jnp.dot(inputs_here, weight_in, preferred_element_type=jnp.float32)
        gate_part = gate_up[:, :F]
        up_part = gate_up[:, F:]
        sigmoid_gate = jax.nn.sigmoid(gate_part)
        hidden = (gate_part * sigmoid_gate * up_part).astype(jnp.bfloat16)
        outputs = jnp.dot(hidden, weight_out, preferred_element_type=jnp.float32).astype(jnp.bfloat16)
        grad_hidden = lax.dot_general(grads_here, weight_out, (((1,), (1,)), ((), ())), preferred_element_type=jnp.float32)
        grad_gate = grad_hidden * up_part * sigmoid_gate * (1.0 + gate_part * (1.0 - sigmoid_gate))
        grad_up = grad_hidden * gate_part * sigmoid_gate
        grad_gate_up = jnp.concatenate([grad_gate, grad_up], axis=1).astype(jnp.bfloat16)
        route_dx = lax.dot_general(grad_gate_up, weight_in, (((1,), (1,)), ((), ())), preferred_element_type=jnp.float32).astype(jnp.bfloat16)
        grouped_in = inputs_here.reshape(EXPERTS, REPLICAS, MOST, D).astype(jnp.float32)
        grouped_dgu = grad_gate_up.reshape(EXPERTS, REPLICAS, MOST, 2 * F).astype(jnp.float32)
        partial_in = jnp.einsum("sdmi,sdmj->dij", grouped_in, grouped_dgu).astype(jnp.bfloat16)
        grad_in = jnp.sum(partial_in.astype(jnp.float32), axis=0).astype(jnp.bfloat16)
        grouped_hidden = hidden.reshape(EXPERTS, REPLICAS, MOST, F).astype(jnp.float32)
        grouped_do = grads_here.reshape(EXPERTS, REPLICAS, MOST, D).astype(jnp.float32)
        partial_out = jnp.einsum("sdmi,sdmj->dij", grouped_hidden, grouped_do).astype(jnp.bfloat16)
        grad_out = jnp.sum(partial_out.astype(jnp.float32), axis=0).astype(jnp.bfloat16)
        return outputs, route_dx, grad_in, grad_out

    outputs, route_dx, grad_in, grad_out = lax.map(expert_pass, jnp.arange(EXPERTS, dtype=jnp.int32))
    flat_index = (positions // MOST) * (blocks * MOST) + block_base * MOST + positions % MOST
    flat_index = flat_index.reshape(-1)
    out_routes = outputs.reshape(-1, D)[flat_index].reshape(TOKENS, TOP, D).astype(jnp.float32)
    mixed = jnp.sum(gates[:, :, None] * out_routes, axis=1).astype(jnp.bfloat16)
    grad_gates = jnp.sum(cotangent[:, None, :].astype(jnp.float32) * out_routes, axis=2)
    dx_routes = route_dx.reshape(-1, D)[flat_index].reshape(TOKENS, TOP, D).astype(jnp.float32)
    grad_tokens = jnp.sum(dx_routes, axis=1).astype(jnp.bfloat16)
    grad_w_in = grad_in.reshape(EXPERTS * D, 2 * F)
    grad_w_out = grad_out.reshape(EXPERTS * F, D)
    return (mixed, grad_tokens, grad_gates, grad_w_in, grad_w_out)
```

```python
import jax
import jax.numpy as jnp
from jax import lax
from jax.experimental import pallas as pl
from jax.experimental.pallas import tpu as pltpu
from jax.sharding import PartitionSpec as P

MESH = pl.DeviceIdType.MESH
BF = jnp.bfloat16
F32 = jnp.float32

D = 4096
F = 768
CAP = 24
SLOTS = 16
ROWS = SLOTS * CAP
TOK = 128
OWN = 12
QD = D // 4
HD = D // 2


def dot(a, b):
    return jnp.dot(a, b, preferred_element_type=F32)


def dot_nt(a, b):
    return lax.dot_general(a, b, (((1,), (1,)), ((), ())), preferred_element_type=F32)


def dot_tn(a, b):
    return lax.dot_general(a, b, (((0,), (0,)), ((), ())), preferred_element_type=F32)


def split_rows(block):
    wide = block.astype(F32)
    n = wide.shape[-1]
    first = wide[:, :CAP, :].reshape(ROWS, n).astype(BF)
    last = wide[:, CAP:, :].reshape(ROWS, n).astype(BF)
    return first, last


def join_rows(first, last):
    n = first.shape[-1]
    s = first.shape[0] // CAP
    return jnp.concatenate([first.reshape(s, CAP, n), last.reshape(s, CAP, n)], axis=1).astype(BF)


def kernel(
    tok_hbm, cot_hbm, routes_ref, gates_ref, win_hbm, wout_hbm,
    mixed_ref, gtok_ref, ggate_ref, gin_ref, gout_ref, ro_hbm, rdx_hbm,
    send, rx, xdz, win, wout, fs, agb, go, gs_in, gr_in, gs_out, gr_out, gt_s, gt_r,
    sel, smat, gcol, stmat, gmat, sval, sret,
    d_ss, d_rs, z_ss, z_rs, a_ss, a_rs, o_ss, o_rs, x_ss, x_rs, s_ss, s_rs, e_ss, e_rs, t_ss, t_rs, loc,
):
    y = lax.axis_index("tensor")
    c = lax.axis_index("context")
    d = lax.axis_index("dp")
    z = d // 2
    xl = d % 2

    def to_expert(i):
        j, m = i // 4, i % 4
        return ((y + 1 + j) % 4, (c + m) % 4, d)

    def to_source(i):
        j, m = i // 4, i % 4
        return ((y + 3 - j) % 4, (c + 4 - m) % 4, d)

    def z_peer(k):
        return (y, c, ((z + k) % 4) * 2 + xl)

    pair = (y, c, z * 2 + (1 - xl))

    def remote(src, dst, ss, rs, dev):
        return pltpu.make_async_remote_copy(
            src_ref=src, dst_ref=dst, send_sem=ss, recv_sem=rs, device_id=dev, device_id_type=MESH
        )

    ld_tok = pltpu.make_async_copy(tok_hbm, mixed_ref, loc.at[0])
    ld_cot = pltpu.make_async_copy(cot_hbm, gtok_ref, loc.at[1])
    ld_win = pltpu.make_async_copy(win_hbm.at[0], win, loc.at[2])
    ld_wout = pltpu.make_async_copy(wout_hbm.at[0], wout, loc.at[3])
    ld_tok.start()
    ld_cot.start()

    bar = pltpu.get_barrier_semaphore()
    for i in range(SLOTS):
        if i != OWN:
            pl.semaphore_signal(bar, inc=1, device_id=to_expert(i), device_id_type=MESH)
    for k in (1, 2, 3):
        pl.semaphore_signal(bar, inc=1, device_id=z_peer(k), device_id_type=MESH)
    pl.semaphore_signal(bar, inc=1, device_id=pair, device_id_type=MESH)

    r0 = routes_ref[0:1, :]
    r1 = routes_ref[1:2, :]
    ids = lax.broadcasted_iota(jnp.int32, (SLOTS, TOK), 0)
    match = jnp.where((ids == r0) | (ids == r1), 1.0, 0.0).astype(BF)
    before = jnp.where(
        lax.broadcasted_iota(jnp.int32, (TOK, TOK), 0) < lax.broadcasted_iota(jnp.int32, (TOK, TOK), 1),
        1.0, 0.0,
    ).astype(BF)
    rank = dot(match, before).astype(BF)
    row = lax.broadcasted_iota(jnp.int32, (ROWS, TOK), 0)
    slot = (row * 683) >> 14
    place = (row - slot * CAP).astype(F32)
    expert = ((y + 1 + (slot >> 2)) & 3) * 4 + ((c + (slot & 3)) & 3)
    pick = jnp.where(
        expert[:, :SLOTS] == lax.broadcasted_iota(jnp.int32, (ROWS, SLOTS), 1), 1.0, 0.0
    ).astype(BF)
    here = dot(pick, rank) == place
    s0 = jnp.where((expert == r0) & here, 1.0, 0.0)
    s1 = jnp.where((expert == r1) & here, 1.0, 0.0)
    sel[0] = s0
    sel[1] = s1
    both = s0 + s1
    smat[...] = both.astype(BF)
    gsel = s0 * gates_ref[0:1, :] + s1 * gates_ref[1:2, :]
    gcol[...] = jnp.broadcast_to(jnp.sum(gsel, axis=1, keepdims=True), (ROWS, TOK))
    stmat[...] = both.T.astype(BF)
    gt = gsel.T
    ghi = gt.astype(BF)
    gmat[0] = ghi
    gmat[1] = (gt - ghi.astype(F32)).astype(BF)

    ld_tok.wait()
    ld_cot.wait()
    ld_win.start()
    ld_wout.start()
    pl.semaphore_wait(bar, 19)

    d_cp = {}
    for j in range(4):
        g0 = j * 4 * CAP

        @pl.loop(0, 4)
        def _(n):
            cs = pl.ds(pl.multiple_of(n * 1024, 1024), 1024)
            sm = smat[g0:g0 + 4 * CAP, :]
            a = dot(sm, mixed_ref[:, cs])
            b = dot(sm, gtok_ref[:, cs]) * gcol[g0:g0 + 4 * CAP, 0:1]
            send[4 * j:4 * j + 4, :, cs] = join_rows(a, b)

        for m in range(4):
            i = 4 * j + m
            if i == OWN:
                d_cp[i] = pltpu.make_async_copy(send.at[i], rx.at[i], loc.at[4])
            else:
                d_cp[i] = remote(send.at[i], rx.at[i], d_ss.at[i], d_rs.at[i], to_expert(i))
            d_cp[i].start()

    z_cp = []
    for j in (3, 0, 2, 1):
        for m in range(4):
            i = 4 * j + m
            if i == OWN:
                d_cp[i].wait()
            else:
                d_cp[i].wait_recv()
        for k in (1, 2, 3):
            n = j * 3 + k - 1
            cols = pl.ds(pl.multiple_of(((z + k) % 4) * QD, QD), QD)
            cp = remote(
                rx.at[4 * j:4 * j + 4, :, cols], xdz.at[k - 1, 4 * j:4 * j + 4],
                z_ss.at[n], z_rs.at[n], z_peer(k),
            )
            cp.start()
            z_cp.append(cp)

    ld_win.wait()
    ld_wout.wait()
    fs[...] = jnp.zeros_like(fs)

    @pl.loop(0, 8)
    def _(n):
        ks = pl.ds(pl.multiple_of(n * 512, 512), 512)
        xk, dk = split_rows(rx[:, :, ks])
        fs[0:ROWS, :] += dot(xk, win[ks, 0:F])
        fs[ROWS:2 * ROWS, :] += dot(xk, win[ks, F:2 * F])
        fs[2 * ROWS:3 * ROWS, :] += dot_nt(dk, wout[:, ks])

    @pl.loop(0, 8)
    def _(n):
        r = pl.multiple_of(n * 48, 48)
        g = fs[pl.ds(r, 48), :]
        u = fs[pl.ds(r + ROWS, 48), :]
        dh = fs[pl.ds(r + 2 * ROWS, 48), :]
        s = jax.nn.sigmoid(g)
        h = (g * s * u).astype(BF)
        rs = pl.ds(r, 48)
        agb[2, 3, rs, :] = h
        agb[0, 3, rs, :] = (dh * u * s * (1.0 + g * (1.0 - s))).astype(BF)
        agb[1, 3, rs, :] = (dh * g * s).astype(BF)
        sval[rs, :] = jnp.broadcast_to(jnp.sum(h.astype(F32) * dh, axis=1, keepdims=True), (48, TOK))

    a_cp = {}
    for p in (2, 0, 1):
        for k in (1, 2, 3):
            n = p * 3 + k - 1
            a_cp[p, k] = remote(agb.at[p, 3], agb.at[p, k - 1], a_ss.at[n], a_rs.at[n], z_peer(k))
            a_cp[p, k].start()

    for i in range(SLOTS):
        if i != OWN:
            d_cp[i].wait_send()

    @pl.loop(0, 4)
    def _(n):
        c0 = pl.multiple_of(n * 512, 512)
        h = agb[2, 3]
        a = dot(h, wout[:, pl.ds(c0, 512)])
        b = dot(h, wout[:, pl.ds(c0 + HD, 512)])
        send[:, :, pl.ds(c0, 512)] = join_rows(a, b)

    o_cp, x_cp, s_cp = {}, {}, {}
    for i in range(SLOTS):
        rows = pl.ds(i * CAP, CAP)
        if i == OWN:
            s_cp[i] = pltpu.make_async_copy(sval.at[rows], sret.at[rows], loc.at[5])
        else:
            o_cp[i] = remote(send.at[i, :, 0:HD], ro_hbm.at[i], o_ss.at[i], o_rs.at[i], to_source(i))
            o_cp[i].start()
            s_cp[i] = remote(sval.at[rows], sret.at[rows], s_ss.at[i], s_rs.at[i], to_source(i))
        s_cp[i].start()

    @pl.loop(0, 4)
    def _(n):
        c0 = pl.multiple_of(n * 512, 512)
        dg = agb[0, 3]
        du = agb[1, 3]
        lo = pl.ds(c0, 512)
        hi = pl.ds(c0 + HD, 512)
        a = dot_nt(dg, win[lo, 0:F]) + dot_nt(du, win[lo, F:2 * F])
        b = dot_nt(dg, win[hi, 0:F]) + dot_nt(du, win[hi, F:2 * F])
        send[:, :, pl.ds(c0 + HD, 512)] = join_rows(a, b)

    for i in range(SLOTS):
        if i != OWN:
            x_cp[i] = remote(send.at[i, :, HD:D], rdx_hbm.at[i], x_ss.at[i], x_rs.at[i], to_source(i))
            x_cp[i].start()

    for cp in z_cp:
        cp.wait()
    own0 = z * QD
    e_cp = []
    for k in (1, 2, 3):
        a_cp[2, k].wait()

    @pl.loop(0, 2)
    def _(n):
        n0 = pl.multiple_of(n * 512, 512)
        acc = None
        for s in range(4):
            if s < 3:
                blk = xdz[s, :, :, pl.ds(n0, 512)]
            else:
                blk = rx[:, :, pl.ds(pl.multiple_of(own0 + n0, 512), 512)]
            _, dk = split_rows(blk)
            t = dot_tn(agb[2, s], dk)
            acc = t if acc is None else acc + t
        go[:, pl.ds(n0, 512)] = acc

    for q in range(4):
        r = pl.multiple_of(q * 192 + (1 - xl) * 96, 96)
        gs_out[q] = go[pl.ds(r, 96), :].astype(BF)
    cp = remote(gs_out, gr_out, e_ss.at[2], e_rs.at[2], pair)
    cp.start()
    e_cp.append(cp)

    for p in range(2):
        for k in (1, 2, 3):
            a_cp[p, k].wait()

        def half(side, store):
            @pl.loop(0, 2)
            def _(n):
                n0 = pl.multiple_of(n * 256, 256)
                acc = None
                for s in range(4):
                    off = pl.multiple_of(side * 512 + n0, 256)
                    if s < 3:
                        blk = xdz[s, :, :, pl.ds(off, 256)]
                    else:
                        blk = rx[:, :, pl.ds(pl.multiple_of(own0 + off, 256), 256)]
                    xk, _ = split_rows(blk)
                    t = dot_tn(xk, agb[p, s])
                    acc = t if acc is None else acc + t
                store(n0, acc)

        def store_send(n0, acc):
            gs_in[p, pl.ds(n0, 256), :] = acc.astype(BF)

        def store_own(n0, acc):
            fs[pl.ds(p * 512 + n0, 256), :] = acc

        half(1 - xl, store_send)
        cp = remote(gs_in.at[p], gr_in.at[p], e_ss.at[p], e_rs.at[p], pair)
        cp.start()
        e_cp.append(cp)
        half(xl, store_own)

    e_cp[0].wait()
    for q in range(4):
        r = pl.multiple_of(q * 192 + xl * 96, 96)
        gt_s[q] = (go[pl.ds(r, 96), :] + gr_out[q].astype(F32)).astype(BF)
    t_cp = []
    for k in (1, 2, 3):
        cp = remote(gt_s.at[(z + k) % 4], gt_r.at[k - 1], t_ss.at[k - 1], t_rs.at[k - 1], z_peer(k))
        cp.start()
        t_cp.append(cp)
    gout_ref[:, pl.ds(pl.multiple_of(own0, QD), QD)] = gt_s[z]

    for i in range(SLOTS):
        if i != OWN:
            s_cp[i].wait()
            o_cp[i].wait()
        else:
            s_cp[i].wait()
    for k in range(2):
        ggate_ref[k:k + 1, :] = (
            jnp.sum(sel[k] * sret[...], axis=0, keepdims=True) / gates_ref[k:k + 1, :]
        )
    back = []
    for i in range(SLOTS):
        src = send.at[i, :, 0:HD] if i == OWN else ro_hbm.at[i]
        back.append(pltpu.make_async_copy(src, rx.at[i, :, 0:HD], loc.at[6 + i]))
        back[-1].start()
    for cp in back:
        cp.wait()

    @pl.loop(0, 4)
    def _(n):
        c0 = pl.multiple_of(n * 512, 512)
        a, b = split_rows(rx[:, :, pl.ds(c0, 512)])
        mixed_ref[:, pl.ds(c0, 512)] = (dot(gmat[0], a) + dot(gmat[1], a)).astype(BF)
        mixed_ref[:, pl.ds(c0 + HD, 512)] = (dot(gmat[0], b) + dot(gmat[1], b)).astype(BF)

    for i in range(SLOTS):
        if i != OWN:
            x_cp[i].wait()
    back = []
    for i in range(SLOTS):
        src = send.at[i, :, HD:D] if i == OWN else rdx_hbm.at[i]
        back.append(pltpu.make_async_copy(src, rx.at[i, :, HD:D], loc.at[6 + i]))
        back[-1].start()
    for cp in back:
        cp.wait()

    @pl.loop(0, 4)
    def _(n):
        c0 = pl.multiple_of(n * 512, 512)
        a, b = split_rows(rx[:, :, pl.ds(c0 + HD, 512)])
        gtok_ref[:, pl.ds(c0, 512)] = dot(stmat[...], a).astype(BF)
        gtok_ref[:, pl.ds(c0 + HD, 512)] = dot(stmat[...], b).astype(BF)

    for p in range(2):
        e_cp[1 + p].wait()
        gin_ref[:, p * F:(p + 1) * F] = (
            fs[p * 512:(p + 1) * 512, :] + gr_in[p].astype(F32)
        ).astype(BF)

    for k in (1, 2, 3):
        t_cp[k - 1].wait()
        col = pl.multiple_of(((z + 4 - k) % 4) * QD, QD)
        gout_ref[:, pl.ds(col, QD)] = gt_r[k - 1]


def shards(tokens, gates, routes, w_in, w_out, cotangent):
    hbm = pl.BlockSpec(memory_space=pl.ANY)
    vm = pl.BlockSpec(memory_space=pltpu.VMEM)
    dma = pltpu.SemaphoreType.DMA
    outs = pl.pallas_call(
        kernel,
        name="experts",
        out_shape=(
            jax.ShapeDtypeStruct((TOK, D), BF),
            jax.ShapeDtypeStruct((TOK, D), BF),
            jax.ShapeDtypeStruct((2, TOK), F32),
            jax.ShapeDtypeStruct((512, 2 * F), BF),
            jax.ShapeDtypeStruct((96, D), BF),
            jax.ShapeDtypeStruct((SLOTS, 48, HD), BF),
            jax.ShapeDtypeStruct((SLOTS, 48, HD), BF),
        ),
        in_specs=[hbm, hbm, vm, vm, hbm, hbm],
        out_specs=(vm, vm, vm, vm, vm, hbm, hbm),
        scratch_shapes=[
            pltpu.VMEM((SLOTS, 48, D), BF),
            pltpu.VMEM((SLOTS, 48, D), BF),
            pltpu.VMEM((3, SLOTS, 48, QD), BF),
            pltpu.VMEM((D, 2 * F), BF),
            pltpu.VMEM((F, D), BF),
            pltpu.VMEM((3 * ROWS, F), F32),
            pltpu.VMEM((3, 4, ROWS, F), BF),
            pltpu.VMEM((F, QD), F32),
            pltpu.VMEM((2, 512, F), BF),
            pltpu.VMEM((2, 512, F), BF),
            pltpu.VMEM((4, 96, QD), BF),
            pltpu.VMEM((4, 96, QD), BF),
            pltpu.VMEM((4, 96, QD), BF),
            pltpu.VMEM((3, 96, QD), BF),
            pltpu.VMEM((2, ROWS, TOK), F32),
            pltpu.VMEM((ROWS, TOK), BF),
            pltpu.VMEM((ROWS, TOK), F32),
            pltpu.VMEM((TOK, ROWS), BF),
            pltpu.VMEM((2, TOK, ROWS), BF),
            pltpu.VMEM((ROWS, TOK), F32),
            pltpu.VMEM((ROWS, TOK), F32),
            dma((SLOTS,)), dma((SLOTS,)),
            dma((12,)), dma((12,)),
            dma((9,)), dma((9,)),
            dma((SLOTS,)), dma((SLOTS,)),
            dma((SLOTS,)), dma((SLOTS,)),
            dma((SLOTS,)), dma((SLOTS,)),
            dma((3,)), dma((3,)),
            dma((3,)), dma((3,)),
            dma((6 + SLOTS,)),
        ],
        compiler_params=pltpu.CompilerParams(
            collective_id=0, has_side_effects=True, vmem_limit_bytes=64 * 2**20 - 65536
        ),
    )(tokens, cotangent, routes.T, gates.T, w_in, w_out)
    return outs[0], outs[1], outs[2].T, outs[3], outs[4]


def solution(mesh):
    rows = P(("tensor", "context", "dp"), None)
    experts = P(("tensor", "context"), None, None)
    return jax.shard_map(
        shards,
        mesh=mesh,
        in_specs=(rows, rows, rows, experts, experts, rows),
        out_specs=(rows, rows, rows, rows, rows),
        check_vma=False,
    )
```

```python
import jax
import jax.numpy as jnp
from jax import lax
from jax.experimental import pallas as pl
from jax.experimental.pallas import tpu as pltpu
from jax.sharding import PartitionSpec as P

MESH = pl.DeviceIdType.MESH
BF = jnp.bfloat16
F32 = jnp.float32

D = 4096
F = 768
CAP = 24
SLOTS = 16
ROWS = SLOTS * CAP
TOK = 128
OWN = 12
ORDER = (2, 1, 3, 0)
QD = D // 4
HD = D // 2


def dot(a, b):
    return jnp.dot(a, b, preferred_element_type=F32)


def dot_nt(a, b):
    return lax.dot_general(a, b, (((1,), (1,)), ((), ())), preferred_element_type=F32)


def dot_tn(a, b):
    return lax.dot_general(a, b, (((0,), (0,)), ((), ())), preferred_element_type=F32)


def split_rows(block):
    wide = block.astype(F32)
    n = wide.shape[-1]
    first = wide[:, :CAP, :].reshape(ROWS, n).astype(BF)
    last = wide[:, CAP:, :].reshape(ROWS, n).astype(BF)
    return first, last


def join_rows(first, last):
    n = first.shape[-1]
    s = first.shape[0] // CAP
    return jnp.concatenate([first.reshape(s, CAP, n), last.reshape(s, CAP, n)], axis=1).astype(BF)


def kernel(
    tok_hbm, cot_hbm, routes_ref, gates_ref, win_hbm, wout_hbm,
    mixed_ref, gtok_ref, ggate_ref, gin_ref, gout_ref, ro_hbm, rdx_hbm,
    send, rx, xdz, win, wout, fs, agb, go, gs_in, gr_in, gs_out, gr_out, gt_s, gt_r,
    sel, smat, gcol, stmat, gmat, sval, sret,
    d_ss, d_rs, z_ss, z_rs, a_ss, a_rs, o_ss, o_rs, x_ss, x_rs, s_ss, s_rs, e_ss, e_rs, t_ss, t_rs, loc,
):
    y = lax.axis_index("tensor")
    c = lax.axis_index("context")
    d = lax.axis_index("dp")
    z = d // 2
    xl = d % 2

    def to_expert(i):
        j, m = i // 4, i % 4
        return ((y + 1 + j) % 4, (c + m) % 4, d)

    def to_source(i):
        j, m = i // 4, i % 4
        return ((y + 3 - j) % 4, (c + 4 - m) % 4, d)

    def z_peer(k):
        return (y, c, ((z + k) % 4) * 2 + xl)

    pair = (y, c, z * 2 + (1 - xl))

    def remote(src, dst, ss, rs, dev):
        return pltpu.make_async_remote_copy(
            src_ref=src, dst_ref=dst, send_sem=ss, recv_sem=rs, device_id=dev, device_id_type=MESH
        )

    ld_tok = pltpu.make_async_copy(tok_hbm, mixed_ref, loc.at[0])
    ld_cot = pltpu.make_async_copy(cot_hbm, gtok_ref, loc.at[1])
    ld_win = pltpu.make_async_copy(win_hbm.at[0], win, loc.at[2])
    ld_wout = pltpu.make_async_copy(wout_hbm.at[0], wout, loc.at[3])
    ld_tok.start()
    ld_cot.start()

    bar = pltpu.get_barrier_semaphore()
    for i in range(SLOTS):
        if i != OWN:
            pl.semaphore_signal(bar, inc=1, device_id=to_expert(i), device_id_type=MESH)
    for k in (1, 2, 3):
        pl.semaphore_signal(bar, inc=1, device_id=z_peer(k), device_id_type=MESH)
    pl.semaphore_signal(bar, inc=1, device_id=pair, device_id_type=MESH)

    r0 = routes_ref[0:1, :]
    r1 = routes_ref[1:2, :]
    ids = lax.broadcasted_iota(jnp.int32, (SLOTS, TOK), 0)
    match = jnp.where((ids == r0) | (ids == r1), 1.0, 0.0).astype(BF)
    before = jnp.where(
        lax.broadcasted_iota(jnp.int32, (TOK, TOK), 0) < lax.broadcasted_iota(jnp.int32, (TOK, TOK), 1),
        1.0, 0.0,
    ).astype(BF)
    rank = dot(match, before).astype(BF)
    row = lax.broadcasted_iota(jnp.int32, (ROWS, TOK), 0)
    slot = (row * 683) >> 14
    place = (row - slot * CAP).astype(F32)
    expert = ((y + 1 + (slot >> 2)) & 3) * 4 + ((c + (slot & 3)) & 3)
    pick = jnp.where(
        expert[:, :SLOTS] == lax.broadcasted_iota(jnp.int32, (ROWS, SLOTS), 1), 1.0, 0.0
    ).astype(BF)
    here = dot(pick, rank) == place
    s0 = jnp.where((expert == r0) & here, 1.0, 0.0)
    s1 = jnp.where((expert == r1) & here, 1.0, 0.0)
    sel[0] = s0
    sel[1] = s1
    both = s0 + s1
    smat[...] = both.astype(BF)
    gsel = s0 * gates_ref[0:1, :] + s1 * gates_ref[1:2, :]
    gcol[...] = jnp.broadcast_to(jnp.sum(gsel, axis=1, keepdims=True), (ROWS, TOK))
    stmat[...] = both.T.astype(BF)
    gt = gsel.T
    ghi = gt.astype(BF)
    gmat[0] = ghi
    gmat[1] = (gt - ghi.astype(F32)).astype(BF)

    ld_tok.wait()
    ld_cot.wait()
    ld_win.start()
    ld_wout.start()
    pl.semaphore_wait(bar, 19)

    def quarter(k):
        return pl.ds(pl.multiple_of(((z + k) % 4) * QD, QD), QD)

    d_cp = {}
    for k in ORDER:

        @pl.loop(0, 2)
        def _(n):
            cs = pl.ds(pl.multiple_of(((z + k) % 4) * QD + n * 512, 512), 512)
            a = dot(smat[...], mixed_ref[:, cs])
            b = dot(smat[...], gtok_ref[:, cs]) * gcol[:, 0:1]
            send[:, :, cs] = join_rows(a, b)

        for i in range(SLOTS):
            src, dst = send.at[i, :, quarter(k)], rx.at[i, :, quarter(k)]
            n = k * SLOTS + i
            if i == OWN:
                d_cp[k, i] = pltpu.make_async_copy(src, dst, loc.at[4 + k])
            else:
                d_cp[k, i] = remote(src, dst, d_ss.at[n], d_rs.at[n], to_expert(i))
            d_cp[k, i].start()

    fs[...] = jnp.zeros_like(fs)
    z_cp = []
    for k in ORDER:
        for i in range(SLOTS):
            if i == OWN:
                d_cp[k, i].wait()
            else:
                d_cp[k, i].wait_recv()
        if k > 0:
            cp = remote(rx.at[:, :, quarter(k)], xdz.at[k - 1], z_ss.at[k - 1], z_rs.at[k - 1], z_peer(k))
            cp.start()
            z_cp.append(cp)
        if k == ORDER[0]:
            ld_win.wait()
            ld_wout.wait()

        @pl.loop(0, 2)
        def _(n):
            ks = pl.ds(pl.multiple_of(((z + k) % 4) * QD + n * 512, 512), 512)
            xk, dk = split_rows(rx[:, :, ks])
            fs[0:ROWS, :] += dot(xk, win[ks, 0:F])
            fs[ROWS:2 * ROWS, :] += dot(xk, win[ks, F:2 * F])
            fs[2 * ROWS:3 * ROWS, :] += dot_nt(dk, wout[:, ks])

    @pl.loop(0, 8)
    def _(n):
        r = pl.multiple_of(n * 48, 48)
        g = fs[pl.ds(r, 48), :]
        u = fs[pl.ds(r + ROWS, 48), :]
        dh = fs[pl.ds(r + 2 * ROWS, 48), :]
        s = jax.nn.sigmoid(g)
        h = (g * s * u).astype(BF)
        rs = pl.ds(r, 48)
        agb[2, 3, rs, :] = h
        agb[0, 3, rs, :] = (dh * u * s * (1.0 + g * (1.0 - s))).astype(BF)
        agb[1, 3, rs, :] = (dh * g * s).astype(BF)
        sval[rs, :] = jnp.broadcast_to(jnp.sum(h.astype(F32) * dh, axis=1, keepdims=True), (48, TOK))

    a_cp = {}
    for p in (2, 0, 1):
        for k in (1, 2, 3):
            n = p * 3 + k - 1
            a_cp[p, k] = remote(agb.at[p, 3], agb.at[p, k - 1], a_ss.at[n], a_rs.at[n], z_peer(k))
            a_cp[p, k].start()

    for k in ORDER:
        for i in range(SLOTS):
            if i != OWN:
                d_cp[k, i].wait_send()

    @pl.loop(0, 4)
    def _(n):
        c0 = pl.multiple_of(n * 512, 512)
        h = agb[2, 3]
        a = dot(h, wout[:, pl.ds(c0, 512)])
        b = dot(h, wout[:, pl.ds(c0 + HD, 512)])
        send[:, :, pl.ds(c0, 512)] = join_rows(a, b)

    o_cp, x_cp, s_cp = {}, {}, {}
    for i in range(SLOTS):
        rows = pl.ds(i * CAP, CAP)
        if i == OWN:
            s_cp[i] = pltpu.make_async_copy(sval.at[rows], sret.at[rows], loc.at[8])
        else:
            o_cp[i] = remote(send.at[i, :, 0:HD], ro_hbm.at[i], o_ss.at[i], o_rs.at[i], to_source(i))
            o_cp[i].start()
            s_cp[i] = remote(sval.at[rows], sret.at[rows], s_ss.at[i], s_rs.at[i], to_source(i))
        s_cp[i].start()

    @pl.loop(0, 4)
    def _(n):
        c0 = pl.multiple_of(n * 512, 512)
        dg = agb[0, 3]
        du = agb[1, 3]
        lo = pl.ds(c0, 512)
        hi = pl.ds(c0 + HD, 512)
        a = dot_nt(dg, win[lo, 0:F]) + dot_nt(du, win[lo, F:2 * F])
        b = dot_nt(dg, win[hi, 0:F]) + dot_nt(du, win[hi, F:2 * F])
        send[:, :, pl.ds(c0 + HD, 512)] = join_rows(a, b)

    for i in range(SLOTS):
        if i != OWN:
            x_cp[i] = remote(send.at[i, :, HD:D], rdx_hbm.at[i], x_ss.at[i], x_rs.at[i], to_source(i))
            x_cp[i].start()

    for cp in z_cp:
        cp.wait()
    own0 = z * QD
    e_cp = []
    for k in (1, 2, 3):
        a_cp[2, k].wait()

    @pl.loop(0, 2)
    def _(n):
        n0 = pl.multiple_of(n * 512, 512)
        acc = None
        for s in range(4):
            if s < 3:
                blk = xdz[s, :, :, pl.ds(n0, 512)]
            else:
                blk = rx[:, :, pl.ds(pl.multiple_of(own0 + n0, 512), 512)]
            _, dk = split_rows(blk)
            t = dot_tn(agb[2, s], dk)
            acc = t if acc is None else acc + t
        go[:, pl.ds(n0, 512)] = acc

    for q in range(4):
        r = pl.multiple_of(q * 192 + (1 - xl) * 96, 96)
        gs_out[q] = go[pl.ds(r, 96), :].astype(BF)
    cp = remote(gs_out, gr_out, e_ss.at[2], e_rs.at[2], pair)
    cp.start()
    e_cp.append(cp)

    for p in range(2):
        for k in (1, 2, 3):
            a_cp[p, k].wait()

        def half(side, store):
            @pl.loop(0, 2)
            def _(n):
                n0 = pl.multiple_of(n * 256, 256)
                acc = None
                for s in range(4):
                    off = pl.multiple_of(side * 512 + n0, 256)
                    if s < 3:
                        blk = xdz[s, :, :, pl.ds(off, 256)]
                    else:
                        blk = rx[:, :, pl.ds(pl.multiple_of(own0 + off, 256), 256)]
                    xk, _ = split_rows(blk)
                    t = dot_tn(xk, agb[p, s])
                    acc = t if acc is None else acc + t
                store(n0, acc)

        def store_send(n0, acc):
            gs_in[p, pl.ds(n0, 256), :] = acc.astype(BF)

        def store_own(n0, acc):
            fs[pl.ds(p * 512 + n0, 256), :] = acc

        half(1 - xl, store_send)
        cp = remote(gs_in.at[p], gr_in.at[p], e_ss.at[p], e_rs.at[p], pair)
        cp.start()
        e_cp.append(cp)
        half(xl, store_own)

    e_cp[0].wait()
    for q in range(4):
        r = pl.multiple_of(q * 192 + xl * 96, 96)
        gt_s[q] = (go[pl.ds(r, 96), :] + gr_out[q].astype(F32)).astype(BF)
    t_cp = []
    for k in (1, 2, 3):
        cp = remote(gt_s.at[(z + k) % 4], gt_r.at[k - 1], t_ss.at[k - 1], t_rs.at[k - 1], z_peer(k))
        cp.start()
        t_cp.append(cp)
    gout_ref[:, pl.ds(pl.multiple_of(own0, QD), QD)] = gt_s[z]

    for i in range(SLOTS):
        if i != OWN:
            s_cp[i].wait()
            o_cp[i].wait()
        else:
            s_cp[i].wait()
    for k in range(2):
        ggate_ref[k:k + 1, :] = (
            jnp.sum(sel[k] * sret[...], axis=0, keepdims=True) / gates_ref[k:k + 1, :]
        )
    back = []
    for i in range(SLOTS):
        src = send.at[i, :, 0:HD] if i == OWN else ro_hbm.at[i]
        back.append(pltpu.make_async_copy(src, rx.at[i, :, 0:HD], loc.at[9 + i]))
        back[-1].start()
    for cp in back:
        cp.wait()

    @pl.loop(0, 4)
    def _(n):
        c0 = pl.multiple_of(n * 512, 512)
        a, b = split_rows(rx[:, :, pl.ds(c0, 512)])
        mixed_ref[:, pl.ds(c0, 512)] = (dot(gmat[0], a) + dot(gmat[1], a)).astype(BF)
        mixed_ref[:, pl.ds(c0 + HD, 512)] = (dot(gmat[0], b) + dot(gmat[1], b)).astype(BF)

    for i in range(SLOTS):
        if i != OWN:
            x_cp[i].wait()
    back = []
    for i in range(SLOTS):
        src = send.at[i, :, HD:D] if i == OWN else rdx_hbm.at[i]
        back.append(pltpu.make_async_copy(src, rx.at[i, :, HD:D], loc.at[9 + i]))
        back[-1].start()
    for cp in back:
        cp.wait()

    @pl.loop(0, 4)
    def _(n):
        c0 = pl.multiple_of(n * 512, 512)
        a, b = split_rows(rx[:, :, pl.ds(c0 + HD, 512)])
        gtok_ref[:, pl.ds(c0, 512)] = dot(stmat[...], a).astype(BF)
        gtok_ref[:, pl.ds(c0 + HD, 512)] = dot(stmat[...], b).astype(BF)

    for p in range(2):
        e_cp[1 + p].wait()
        gin_ref[:, p * F:(p + 1) * F] = (
            fs[p * 512:(p + 1) * 512, :] + gr_in[p].astype(F32)
        ).astype(BF)

    for k in (1, 2, 3):
        t_cp[k - 1].wait()
        col = pl.multiple_of(((z + 4 - k) % 4) * QD, QD)
        gout_ref[:, pl.ds(col, QD)] = gt_r[k - 1]


def shards(tokens, gates, routes, w_in, w_out, cotangent):
    hbm = pl.BlockSpec(memory_space=pl.ANY)
    vm = pl.BlockSpec(memory_space=pltpu.VMEM)
    dma = pltpu.SemaphoreType.DMA
    outs = pl.pallas_call(
        kernel,
        name="experts",
        out_shape=(
            jax.ShapeDtypeStruct((TOK, D), BF),
            jax.ShapeDtypeStruct((TOK, D), BF),
            jax.ShapeDtypeStruct((2, TOK), F32),
            jax.ShapeDtypeStruct((512, 2 * F), BF),
            jax.ShapeDtypeStruct((96, D), BF),
            jax.ShapeDtypeStruct((SLOTS, 48, HD), BF),
            jax.ShapeDtypeStruct((SLOTS, 48, HD), BF),
        ),
        in_specs=[hbm, hbm, vm, vm, hbm, hbm],
        out_specs=(vm, vm, vm, vm, vm, hbm, hbm),
        scratch_shapes=[
            pltpu.VMEM((SLOTS, 48, D), BF),
            pltpu.VMEM((SLOTS, 48, D), BF),
            pltpu.VMEM((3, SLOTS, 48, QD), BF),
            pltpu.VMEM((D, 2 * F), BF),
            pltpu.VMEM((F, D), BF),
            pltpu.VMEM((3 * ROWS, F), F32),
            pltpu.VMEM((3, 4, ROWS, F), BF),
            pltpu.VMEM((F, QD), F32),
            pltpu.VMEM((2, 512, F), BF),
            pltpu.VMEM((2, 512, F), BF),
            pltpu.VMEM((4, 96, QD), BF),
            pltpu.VMEM((4, 96, QD), BF),
            pltpu.VMEM((4, 96, QD), BF),
            pltpu.VMEM((3, 96, QD), BF),
            pltpu.VMEM((2, ROWS, TOK), F32),
            pltpu.VMEM((ROWS, TOK), BF),
            pltpu.VMEM((ROWS, TOK), F32),
            pltpu.VMEM((TOK, ROWS), BF),
            pltpu.VMEM((2, TOK, ROWS), BF),
            pltpu.VMEM((ROWS, TOK), F32),
            pltpu.VMEM((ROWS, TOK), F32),
            dma((4 * SLOTS,)), dma((4 * SLOTS,)),
            dma((3,)), dma((3,)),
            dma((9,)), dma((9,)),
            dma((SLOTS,)), dma((SLOTS,)),
            dma((SLOTS,)), dma((SLOTS,)),
            dma((SLOTS,)), dma((SLOTS,)),
            dma((3,)), dma((3,)),
            dma((3,)), dma((3,)),
            dma((9 + SLOTS,)),
        ],
        compiler_params=pltpu.CompilerParams(
            collective_id=0, has_side_effects=True, vmem_limit_bytes=64 * 2**20 - 65536
        ),
    )(tokens, cotangent, routes.T, gates.T, w_in, w_out)
    return outs[0], outs[1], outs[2].T, outs[3], outs[4]


def solution(mesh):
    rows = P(("tensor", "context", "dp"), None)
    experts = P(("tensor", "context"), None, None)
    return jax.shard_map(
        shards,
        mesh=mesh,
        in_specs=(rows, rows, rows, experts, experts, rows),
        out_specs=(rows, rows, rows, rows, rows),
        check_vma=False,
    )
```

```python
import jax
import jax.numpy as jnp
from jax import lax
from jax.experimental import pallas as pl
from jax.experimental.pallas import tpu as pltpu
from jax.sharding import PartitionSpec as P

MESH = pl.DeviceIdType.MESH
BF = jnp.bfloat16
F32 = jnp.float32

D = 4096
F = 768
CAP = 24
SLOTS = 16
ROWS = SLOTS * CAP
TOK = 128
OWN = 12
PIECES = ((2, 0, 1024), (1, 0, 1024), (3, 0, 1024), (0, 0, 1024))
QD = D // 4
HD = D // 2


def dot(a, b):
    return jnp.dot(a, b, preferred_element_type=F32)


def dot_nt(a, b):
    return lax.dot_general(a, b, (((1,), (1,)), ((), ())), preferred_element_type=F32)


def dot_tn(a, b):
    return lax.dot_general(a, b, (((0,), (0,)), ((), ())), preferred_element_type=F32)


def split_rows(block):
    wide = block.astype(F32)
    n = wide.shape[-1]
    first = wide[:, :CAP, :].reshape(ROWS, n).astype(BF)
    last = wide[:, CAP:, :].reshape(ROWS, n).astype(BF)
    return first, last


def join_rows(first, last):
    n = first.shape[-1]
    s = first.shape[0] // CAP
    return jnp.concatenate([first.reshape(s, CAP, n), last.reshape(s, CAP, n)], axis=1).astype(BF)


def kernel(
    tok_hbm, cot_hbm, routes_ref, gates_ref, win_hbm, wout_hbm,
    mixed_out, gtok_out, ggate_ref, gin_out, gout_out, ro_hbm, rdx_hbm,
    mixed_ref, gtok_ref, gin_ref, gout_ref,
    send, rx, xdz, win, wout, fs, agb, go, gr_in, gr_out, gt_r, pr,
    sel, smat, pack_s, pack_r, gcol, stmat, gmat, sval, sret,
    d_ss, d_rs, z_ss, z_rs, a_ss, a_rs, o_ss, o_rs, x_ss, x_rs, s_ss, s_rs, e_ss, e_rs, t_ss, t_rs,
    g_ss, g_rs, p_ss, p_rs, loc, out_sem,
):
    y = lax.axis_index("tensor")
    c = lax.axis_index("context")
    d = lax.axis_index("dp")
    z = d // 2
    xl = d % 2
    xh = c // 2
    co = c % 2

    def context_of(i):
        return (1 - xh if i % 2 else xh) * 2 + (1 - co if i // 2 % 2 else co)

    def to_expert(i):
        return ((y + 1 + i // 4) % 4, context_of(i), d)

    def to_source(i):
        return ((y + 3 - i // 4) % 4, context_of(i), d)

    def z_peer(k):
        return (y, c, ((z + k) % 4) * 2 + xl)

    pair = (y, c, z * 2 + (1 - xl))
    partner = to_expert(OWN + 1)

    def remote(src, dst, ss, rs, dev):
        return pltpu.make_async_remote_copy(
            src_ref=src, dst_ref=dst, send_sem=ss, recv_sem=rs, device_id=dev, device_id_type=MESH
        )

    ld_tok = pltpu.make_async_copy(tok_hbm, mixed_ref, loc.at[0])
    ld_cot = pltpu.make_async_copy(cot_hbm, gtok_ref, loc.at[1])
    ld_win = pltpu.make_async_copy(win_hbm.at[0], win, loc.at[2])
    ld_wout = pltpu.make_async_copy(wout_hbm.at[0], wout, loc.at[3])
    ld_tok.start()
    ld_cot.start()

    bar = pltpu.get_barrier_semaphore()
    for i in range(SLOTS):
        if i != OWN:
            pl.semaphore_signal(bar, inc=1, device_id=to_expert(i), device_id_type=MESH)
    for k in (1, 2, 3):
        pl.semaphore_signal(bar, inc=1, device_id=z_peer(k), device_id_type=MESH)
    pl.semaphore_signal(bar, inc=1, device_id=pair, device_id_type=MESH)

    pack_s[0:2, :] = routes_ref[...].astype(F32)
    pack_s[2:4, :] = gates_ref[...]
    row = lax.broadcasted_iota(jnp.int32, (ROWS, TOK), 0)
    slot = (row * 683) >> 14
    place = (row - slot * CAP).astype(F32)
    far = slot & 1
    ahead = ((y + 1 + (slot >> 2)) & 3) * 4 + (co ^ ((slot >> 1) & 1))
    before = jnp.where(
        lax.broadcasted_iota(jnp.int32, (TOK, TOK), 0) < lax.broadcasted_iota(jnp.int32, (TOK, TOK), 1),
        1.0, 0.0,
    ).astype(BF)

    def tables(pack, half):
        r0, r1 = pack[0:1, :], pack[1:2, :]
        expert = (ahead + (half ^ far) * 2).astype(F32)
        ids = lax.broadcasted_iota(jnp.int32, (SLOTS, TOK), 0).astype(F32)
        match = jnp.where((ids == r0) | (ids == r1), 1.0, 0.0).astype(BF)
        rank = dot(match, before).astype(BF)
        pick = jnp.where(
            expert[:, :SLOTS] == lax.broadcasted_iota(jnp.int32, (ROWS, SLOTS), 1).astype(F32), 1.0, 0.0
        ).astype(BF)
        here = dot(pick, rank) == place
        s0 = jnp.where((expert == r0) & here, 1.0, 0.0)
        s1 = jnp.where((expert == r1) & here, 1.0, 0.0)
        return s0, s1, s0 * pack[2:3, :] + s1 * pack[3:4, :]

    s0, s1, gsel = tables(pack_s[...], xh)
    sel[0] = s0
    sel[1] = s1
    smat[...] = (s0 + s1).astype(BF)
    gcol[...] = jnp.broadcast_to(jnp.sum(gsel, axis=1, keepdims=True), (ROWS, TOK))

    def put(half, gates, chosen):
        rows = pl.ds(half * TOK, TOK)
        gt = gates.T
        ghi = gt.astype(BF)
        gmat[0, rows, :] = ghi
        gmat[1, rows, :] = (gt - ghi.astype(F32)).astype(BF)
        stmat[rows, :] = chosen.T.astype(BF)

    ld_tok.wait()
    ld_cot.wait()
    ld_win.start()
    ld_wout.start()
    pl.semaphore_wait(bar, 19)

    g_cp = remote(pack_s, pack_r, g_ss.at[0], g_rs.at[0], partner)
    g_cp.start()

    def quarter(k, off, width):
        return pl.ds(pl.multiple_of(((z + k) % 4) * QD + off, 512), width)

    d_cp = {}
    for u, (k, off, width) in enumerate(PIECES):

        @pl.loop(0, width // 512)
        def _(n):
            cs = pl.ds(pl.multiple_of(((z + k) % 4) * QD + off + n * 512, 512), 512)
            a = dot(smat[...], mixed_ref[:, cs])
            b = dot(smat[...], gtok_ref[:, cs]) * gcol[:, 0:1]
            send[:, :, cs] = join_rows(a, b)

        cols = quarter(k, off, width)
        for i in range(SLOTS):
            src, dst = send.at[i, :, cols], rx.at[i, :, cols]
            n = u * SLOTS + i
            if i == OWN:
                d_cp[u, i] = pltpu.make_async_copy(src, dst, loc.at[4 + u])
            else:
                d_cp[u, i] = remote(src, dst, d_ss.at[n], d_rs.at[n], to_expert(i))
            d_cp[u, i].start()

    fs[...] = jnp.zeros_like(fs)
    near = far == 0
    put(
        0, jnp.where(near, sel[0] * pack_s[2:3, :] + sel[1] * pack_s[3:4, :], 0.0),
        jnp.where(near, sel[0] + sel[1], 0.0),
    )
    g_cp.wait()
    t0, t1, tsel = tables(pack_r[...], 1 - xh)
    put(1, jnp.where(near, 0.0, tsel), jnp.where(near, 0.0, t0 + t1))
    z_cp = []
    for u, (k, off, width) in enumerate(PIECES):
        for i in range(SLOTS):
            if i == OWN:
                d_cp[u, i].wait()
            else:
                d_cp[u, i].wait_recv()
        if k > 0:
            cp = remote(
                rx.at[:, :, quarter(k, off, width)], xdz.at[k - 1, :, :, pl.ds(off, width)],
                z_ss.at[u], z_rs.at[u], z_peer(k),
            )
            cp.start()
            z_cp.append(cp)
        if u == 0:
            ld_win.wait()
            ld_wout.wait()

        @pl.loop(0, width // 512)
        def _(n):
            ks = pl.ds(pl.multiple_of(((z + k) % 4) * QD + off + n * 512, 512), 512)
            xk, dk = split_rows(rx[:, :, ks])
            fs[0:ROWS, :] += dot(xk, win[ks, 0:F])
            fs[ROWS:2 * ROWS, :] += dot(xk, win[ks, F:2 * F])
            fs[2 * ROWS:3 * ROWS, :] += dot_nt(dk, wout[:, ks])

    @pl.loop(0, 8)
    def _(n):
        r = pl.multiple_of(n * 48, 48)
        g = fs[pl.ds(r, 48), :]
        u = fs[pl.ds(r + ROWS, 48), :]
        dh = fs[pl.ds(r + 2 * ROWS, 48), :]
        s = jax.nn.sigmoid(g)
        h = (g * s * u).astype(BF)
        rs = pl.ds(r, 48)
        agb[2, 3, rs, :] = h
        agb[0, 3, rs, :] = (dh * u * s * (1.0 + g * (1.0 - s))).astype(BF)
        agb[1, 3, rs, :] = (dh * g * s).astype(BF)
        sval[rs, :] = jnp.broadcast_to(jnp.sum(h.astype(F32) * dh, axis=1, keepdims=True), (48, TOK))

    a_cp = {}

    def gather_start(p):
        for k in (1, 3):
            n = p * 4 + k
            a_cp[p, k] = remote(agb.at[p, 3], agb.at[p, k - 1], a_ss.at[n], a_rs.at[n], z_peer(k))
            a_cp[p, k].start()

    def gather_pass(p):
        for k, cols in ((1, pl.ds(0, F // 2)), (3, pl.ds(F // 2, F // 2))):
            a_cp[p, k].wait_recv()
            n = p * 4 + k - 1
            a_cp[p, k - 1] = remote(
                agb.at[p, k - 1, :, cols], agb.at[p, 1, :, cols], a_ss.at[n], a_rs.at[n], z_peer(k)
            )
            a_cp[p, k - 1].start()

    def gather_end(p):
        a_cp[p, 0].wait_recv()
        a_cp[p, 2].wait_recv()

    gather_start(2)
    gather_start(0)

    for u in range(len(PIECES)):
        for i in range(SLOTS):
            if i != OWN:
                d_cp[u, i].wait_send()

    o_cp, s_cp = {}, {}

    def give(t, q, buf, ss, rs):
        cols = pl.ds(q * QD, QD)
        for p in range(8):
            src, dst = send.at[8 * t + p, :, cols], buf.at[pl.ds(p * 48, 48), cols]
            n = q * 8 + p
            if 2 * p == OWN:
                cp = pltpu.make_async_copy(src, dst, loc.at[11 + 4 * t + q])
            else:
                cp = remote(src, dst, ss.at[n], rs.at[n], to_source(2 * p))
            cp.start()
            o_cp[t, q, p] = cp

    for q in range(4):

        @pl.loop(0, 2)
        def _(n):
            cs = pl.ds(pl.multiple_of(q * QD + n * 512, 512), 512)
            send[0:8, :, cs] = dot(agb[2, 3], wout[:, cs]).astype(BF).reshape(8, 48, 512)

        give(0, q, ro_hbm, o_ss, o_rs)

    for i in range(SLOTS):
        rows = pl.ds(i * CAP, CAP)
        if i == OWN:
            s_cp[i] = pltpu.make_async_copy(sval.at[rows], sret.at[rows], loc.at[10])
        else:
            s_cp[i] = remote(sval.at[rows], sret.at[rows], s_ss.at[i], s_rs.at[i], to_source(i))
        s_cp[i].start()

    for q in range(4):

        @pl.loop(0, 2)
        def _(n):
            cs = pl.ds(pl.multiple_of(q * QD + n * 512, 512), 512)
            dx = dot_nt(agb[0, 3], win[cs, 0:F]) + dot_nt(agb[1, 3], win[cs, F:2 * F])
            send[8:16, :, cs] = dx.astype(BF).reshape(8, 48, 512)

        give(1, q, rdx_hbm, x_ss, x_rs)

    p_cp = {}

    def relay(t, q):
        cols = pl.ds(q * QD, QD)
        buf = rdx_hbm if t else ro_hbm
        for p in range(8):
            if 2 * p == OWN:
                o_cp[t, q, p].wait()
            else:
                o_cp[t, q, p].wait_recv()
        ld = pltpu.make_async_copy(buf.at[:, cols], wout.at[256:640, cols], loc.at[19 + 4 * t + q])
        ld.start()
        ld.wait()
        own = gtok_ref if t else mixed_ref

        @pl.loop(0, 2)
        def _(n):
            cs = pl.ds(pl.multiple_of(q * QD + n * 512, 512), 512)
            rows = wout[256:640, cs]
            if t:
                part = dot(stmat[...], rows)
            else:
                part = dot(gmat[0], rows) + dot(gmat[1], rows)
            own[:, cs] = part[0:TOK].astype(BF)
            wout[TOK * t:TOK * (t + 1), cs] = part[TOK:2 * TOK].astype(BF)

        n = 4 * t + q
        p_cp[t, q] = remote(
            wout.at[TOK * t:TOK * (t + 1), cols], pr.at[t, :, cols], p_ss.at[n], p_rs.at[n], partner
        )
        p_cp[t, q].start()

    own0 = z * QD
    e_cp = {}
    GS = 512
    GT = 896

    DC = 1280
    XT = 2816

    def arrange():
        for cp in z_cp:
            cp.wait()
        for s in range(4):

            @pl.loop(0, 4)
            def _(n):
                n0 = pl.multiple_of(n * 256, 256)
                if s < 3:
                    blk = xdz[s, :, :, pl.ds(n0, 256)]
                else:
                    blk = rx[:, :, pl.ds(pl.multiple_of(own0 + n0, 256), 256)]
                xk, dk = split_rows(blk)
                win[DC + s * ROWS:DC + (s + 1) * ROWS, pl.ds(n0, 256)] = dk
                win[pl.ds(XT + n0, 256), s * ROWS:(s + 1) * ROWS] = xk.T

    def grad_out():
        gather_end(2)

        @pl.loop(0, 3)
        def _(n):
            n0 = pl.multiple_of(n * 256, 256)
            h = agb[2, :, :, pl.ds(n0, 256)].reshape(4 * ROWS, 256)
            go[pl.ds(n0, 256), :] = dot_tn(h, win[DC:DC + 4 * ROWS, 0:QD])

        for q in range(4):
            r = pl.multiple_of(q * 192 + (1 - xl) * 96, 96)
            win[GS + q * 96:GS + (q + 1) * 96, 0:QD] = go[pl.ds(r, 96), :].astype(BF)
        e_cp[2] = remote(win.at[GS:GS + 384, 0:QD], gr_out, e_ss.at[2], e_rs.at[2], pair)
        e_cp[2].start()

    def grad_in(p):
        gather_end(p)

        def half(side, store):
            @pl.loop(0, 2)
            def _(n):
                n0 = pl.multiple_of(n * 256, 256)
                r = pl.multiple_of(XT + side * 512 + n0, 256)
                store(n0, dot(win[pl.ds(r, 256), :], agb[p].reshape(4 * ROWS, F)))

        def store_send(n0, acc):
            win[pl.ds(n0, 256), p * F:(p + 1) * F] = acc.astype(BF)

        def store_own(n0, acc):
            fs[pl.ds(p * 512 + n0, 256), :] = acc

        half(1 - xl, store_send)
        e_cp[p] = remote(win.at[0:512, p * F:(p + 1) * F], gr_in.at[p], e_ss.at[p], e_rs.at[p], pair)
        e_cp[p].start()
        half(xl, store_own)

    t_cp = []

    def out_rows():
        e_cp[2].wait()
        for q in range(4):
            r = pl.multiple_of(q * 192 + xl * 96, 96)
            win[GT + q * 96:GT + (q + 1) * 96, 0:QD] = (
                go[pl.ds(r, 96), :] + gr_out[q * 96:(q + 1) * 96, :].astype(F32)
            ).astype(BF)
        for k in (1, 2, 3):
            r = pl.multiple_of(GT + ((z + k) % 4) * 96, 32)
            cp = remote(
                win.at[pl.ds(r, 96), 0:QD], gt_r.at[k - 1], t_ss.at[k - 1], t_rs.at[k - 1], z_peer(k)
            )
            cp.start()
            t_cp.append(cp)
        gout_ref[:, pl.ds(pl.multiple_of(own0, QD), QD)] = win[pl.ds(pl.multiple_of(GT + z * 96, 32), 96), 0:QD]

    relay(0, 0)
    relay(0, 1)
    gather_pass(2)
    gather_start(1)
    relay(0, 2)
    relay(0, 3)
    gather_pass(0)
    relay(1, 0)
    arrange()
    grad_out()
    relay(1, 1)
    gather_pass(1)
    relay(1, 2)
    grad_in(0)
    relay(1, 3)
    grad_in(1)
    out_rows()

    for i in range(SLOTS):
        s_cp[i].wait()
    for k in range(2):
        ggate_ref[k:k + 1, :] = (
            jnp.sum(sel[k] * sret[...], axis=0, keepdims=True) / gates_ref[k:k + 1, :]
        )
    out_cp = []

    def leave(src, dst):
        cp = pltpu.make_async_copy(src, dst, out_sem.at[len(out_cp)])
        cp.start()
        out_cp.append(cp)

    for k in (1, 2, 3):
        t_cp[k - 1].wait()
        col = pl.multiple_of(((z + 4 - k) % 4) * QD, QD)
        gout_ref[:, pl.ds(col, QD)] = gt_r[k - 1]
    leave(gout_ref, gout_out)
    for t in range(2):
        own = gtok_ref if t else mixed_ref
        for q in range(4):
            p_cp[t, q].wait()
            cs = pl.ds(q * QD, QD)
            own[:, cs] = (own[:, cs].astype(F32) + pr[t, :, cs].astype(F32)).astype(BF)
        leave(own, gtok_out if t else mixed_out)
    for p in range(2):
        e_cp[p].wait()
        cs = pl.ds(p * F, F)
        gin_ref[:, cs] = (fs[p * 512:(p + 1) * 512, :] + gr_in[p].astype(F32)).astype(BF)
        leave(gin_ref.at[:, cs], gin_out.at[:, cs])

    for p in range(3):
        for k in range(4):
            a_cp[p, k].wait_send()
    for t in range(2):
        for q in range(4):
            for p in range(8):
                if 2 * p != OWN:
                    o_cp[t, q, p].wait_send()
    for cp in out_cp:
        cp.wait()


def hand_over(*refs):
    ins, outs, held, sems = refs[:5], refs[5:10], refs[10:15], refs[15]
    loads = [pltpu.make_async_copy(ins[n], held[n], sems.at[n]) for n in range(5)]
    stores = [pltpu.make_async_copy(held[n], outs[n], sems.at[5 + n]) for n in range(5)]
    for cp in loads:
        cp.start()
    for n in range(5):
        loads[n].wait()
        stores[n].start()
    for cp in stores:
        cp.wait()


def shards(tokens, gates, routes, w_in, w_out, cotangent):
    hbm = pl.BlockSpec(memory_space=pl.ANY)
    vm = pl.BlockSpec(memory_space=pltpu.VMEM)
    dma = pltpu.SemaphoreType.DMA
    outs = pl.pallas_call(
        kernel,
        name="experts",
        out_shape=(
            jax.ShapeDtypeStruct((TOK, D), BF),
            jax.ShapeDtypeStruct((TOK, D), BF),
            jax.ShapeDtypeStruct((2, TOK), F32),
            jax.ShapeDtypeStruct((512, 2 * F), BF),
            jax.ShapeDtypeStruct((96, D), BF),
            jax.ShapeDtypeStruct((ROWS, D), BF),
            jax.ShapeDtypeStruct((ROWS, D), BF),
        ),
        in_specs=[hbm, hbm, vm, vm, hbm, hbm],
        out_specs=(hbm, hbm, vm, hbm, hbm, hbm, hbm),
        scratch_shapes=[
            pltpu.VMEM((TOK, D), BF),
            pltpu.VMEM((TOK, D), BF),
            pltpu.VMEM((512, 2 * F), BF),
            pltpu.VMEM((96, D), BF),
            pltpu.VMEM((SLOTS, 48, D), BF),
            pltpu.VMEM((SLOTS, 48, D), BF),
            pltpu.VMEM((3, SLOTS, 48, QD), BF),
            pltpu.VMEM((D, 2 * F), BF),
            pltpu.VMEM((F, D), BF),
            pltpu.VMEM((3 * ROWS, F), F32),
            pltpu.VMEM((3, 4, ROWS, F), BF),
            pltpu.VMEM((F, QD), F32),
            pltpu.VMEM((2, 512, F), BF),
            pltpu.VMEM((384, QD), BF),
            pltpu.VMEM((3, 96, QD), BF),
            pltpu.VMEM((2, TOK, D), BF),
            pltpu.VMEM((2, ROWS, TOK), F32),
            pltpu.VMEM((ROWS, TOK), BF),
            pltpu.VMEM((8, TOK), F32),
            pltpu.VMEM((8, TOK), F32),
            pltpu.VMEM((ROWS, TOK), F32),
            pltpu.VMEM((2 * TOK, ROWS), BF),
            pltpu.VMEM((2, 2 * TOK, ROWS), BF),
            pltpu.VMEM((ROWS, TOK), F32),
            pltpu.VMEM((ROWS, TOK), F32),
            dma((len(PIECES) * SLOTS,)), dma((len(PIECES) * SLOTS,)),
            dma((len(PIECES),)), dma((len(PIECES),)),
            dma((12,)), dma((12,)),
            dma((32,)), dma((32,)),
            dma((32,)), dma((32,)),
            dma((SLOTS,)), dma((SLOTS,)),
            dma((3,)), dma((3,)),
            dma((3,)), dma((3,)),
            dma((1,)), dma((1,)),
            dma((8,)), dma((8,)),
            dma((27,)),
            dma((5,)),
        ],
        compiler_params=pltpu.CompilerParams(
            collective_id=0, has_side_effects=True, vmem_limit_bytes=64 * 2**20 - 65536
        ),
    )(tokens, cotangent, routes.T, gates.T, w_in, w_out)
    outs = pl.pallas_call(
        hand_over,
        name="hand_over",
        out_shape=tuple(jax.ShapeDtypeStruct(o.shape, o.dtype) for o in outs[:5]),
        in_specs=[hbm] * 5,
        out_specs=(hbm,) * 5,
        scratch_shapes=[pltpu.VMEM(o.shape, o.dtype) for o in outs[:5]] + [dma((10,))],
    )(*outs[:5])
    return outs[0], outs[1], outs[2].T, outs[3], outs[4]


def solution(mesh):
    rows = P(("tensor", "context", "dp"), None)
    experts = P(("tensor", "context"), None, None)
    return jax.shard_map(
        shards,
        mesh=mesh,
        in_specs=(rows, rows, rows, experts, experts, rows),
        out_specs=(rows, rows, rows, rows, rows),
        check_vma=False,
    )
```

```python
import jax
import jax.numpy as jnp
from jax import lax
from jax.experimental import pallas as pl
from jax.experimental.pallas import tpu as pltpu
from jax.sharding import PartitionSpec as P

MESH = pl.DeviceIdType.MESH
BF = jnp.bfloat16
F32 = jnp.float32

D = 4096
F = 768
CAP = 24
SLOTS = 16
ROWS = SLOTS * CAP
TOK = 128
OWN = 6
PIECES = ((2, 0, 1024), (1, 0, 1024), (3, 0, 1024), (0, 0, 1024))
QD = D // 4
HD = D // 2


def dot(a, b):
    return jnp.dot(a, b, preferred_element_type=F32)


def dot_nt(a, b):
    return lax.dot_general(a, b, (((1,), (1,)), ((), ())), preferred_element_type=F32)


def dot_tn(a, b):
    return lax.dot_general(a, b, (((0,), (0,)), ((), ())), preferred_element_type=F32)


def split_rows(block):
    wide = block.astype(F32)
    rows, n = wide.shape[0] * CAP, wide.shape[-1]
    first = wide[:, :CAP, :].reshape(rows, n).astype(BF)
    last = wide[:, CAP:, :].reshape(rows, n).astype(BF)
    return first, last


def join_rows(first, last):
    n = first.shape[-1]
    s = first.shape[0] // CAP
    return jnp.concatenate([first.reshape(s, CAP, n), last.reshape(s, CAP, n)], axis=1).astype(BF)


def kernel(
    tok_hbm, cot_hbm, routes_ref, gates_ref, win_hbm, wout_hbm,
    mixed_out, gtok_out, ggate_ref, gin_out, gout_out, ro_hbm,
    mixed_ref, gtok_ref, gin_ref, gout_ref,
    send, rx, xdz, win, wout, fs, agb, go, gr_in, gr_out, gt_r, pr,
    sel, smat, pack_s, pack_r, gcol, stmat, gmat, sval, sret,
    d_ss, d_rs, z_ss, z_rs, a_ss, a_rs, o_ss, o_rs, s_ss, s_rs, e_ss, e_rs, t_ss, t_rs,
    g_ss, g_rs, p_ss, p_rs, loc, out_sem,
):
    y = lax.axis_index("tensor")
    c = lax.axis_index("context")
    d = lax.axis_index("dp")
    z = d // 2
    xl = d % 2
    xh = c // 2
    co = c % 2

    def context_of(i):
        return (1 - xh if i // 8 else xh) * 2 + (1 - co if i % 2 else co)

    def to_expert(i):
        return ((y + 1 + i % 8 // 2) % 4, context_of(i), d)

    def to_source(i):
        return ((y + 3 - i % 8 // 2) % 4, context_of(i), d)

    def z_peer(k):
        return (y, c, ((z + k) % 4) * 2 + xl)

    pair = (y, c, z * 2 + (1 - xl))
    partner = to_expert(OWN + 8)

    def remote(src, dst, ss, rs, dev):
        return pltpu.make_async_remote_copy(
            src_ref=src, dst_ref=dst, send_sem=ss, recv_sem=rs, device_id=dev, device_id_type=MESH
        )

    ld_tok = pltpu.make_async_copy(tok_hbm, mixed_ref, loc.at[0])
    ld_cot = pltpu.make_async_copy(cot_hbm, gtok_ref, loc.at[1])
    ld_win = pltpu.make_async_copy(win_hbm.at[0], win, loc.at[2])
    ld_wout = pltpu.make_async_copy(wout_hbm.at[0], wout, loc.at[3])
    ld_tok.start()
    ld_cot.start()

    bar = pltpu.get_barrier_semaphore()
    for i in range(SLOTS):
        if i != OWN:
            pl.semaphore_signal(bar, inc=1, device_id=to_expert(i), device_id_type=MESH)
    for k in (1, 2, 3):
        pl.semaphore_signal(bar, inc=1, device_id=z_peer(k), device_id_type=MESH)
    pl.semaphore_signal(bar, inc=1, device_id=pair, device_id_type=MESH)

    pack_s[0:2, :] = routes_ref[...].astype(F32)
    pack_s[2:4, :] = gates_ref[...]
    row = lax.broadcasted_iota(jnp.int32, (ROWS, TOK), 0)
    slot = (row * 683) >> 14
    place = (row - slot * CAP).astype(F32)
    far = slot >> 3
    ahead = ((y + 1 + ((slot >> 1) & 3)) & 3) * 4 + (co ^ (slot & 1))
    before = jnp.where(
        lax.broadcasted_iota(jnp.int32, (TOK, TOK), 0) < lax.broadcasted_iota(jnp.int32, (TOK, TOK), 1),
        1.0, 0.0,
    ).astype(BF)

    def tables(pack, half):
        r0, r1 = pack[0:1, :], pack[1:2, :]
        expert = (ahead + (half ^ far) * 2).astype(F32)
        ids = lax.broadcasted_iota(jnp.int32, (SLOTS, TOK), 0).astype(F32)
        match = jnp.where((ids == r0) | (ids == r1), 1.0, 0.0).astype(BF)
        rank = dot(match, before).astype(BF)
        pick = jnp.where(
            expert[:, :SLOTS] == lax.broadcasted_iota(jnp.int32, (ROWS, SLOTS), 1).astype(F32), 1.0, 0.0
        ).astype(BF)
        here = dot(pick, rank) == place
        s0 = jnp.where((expert == r0) & here, 1.0, 0.0)
        s1 = jnp.where((expert == r1) & here, 1.0, 0.0)
        return s0, s1, s0 * pack[2:3, :] + s1 * pack[3:4, :]

    s0, s1, gsel = tables(pack_s[...], xh)
    sel[0] = s0
    sel[1] = s1
    smat[...] = (s0 + s1).astype(BF)
    gcol[...] = jnp.broadcast_to(jnp.sum(gsel, axis=1, keepdims=True), (ROWS, TOK))

    HALF = ROWS // 2

    def put(half, gates, chosen):
        rows = pl.ds(half * TOK, TOK)
        cut = slice(half * HALF, (half + 1) * HALF)
        gt = gates.T
        ghi = gt.astype(BF)
        gmat[0, rows, :] = ghi[:, cut]
        gmat[1, rows, :] = (gt - ghi.astype(F32)).astype(BF)[:, cut]
        stmat[rows, :] = chosen.T.astype(BF)[:, cut]

    ld_tok.wait()
    ld_cot.wait()
    ld_win.start()
    ld_wout.start()
    pl.semaphore_wait(bar, 19)

    g_cp = remote(pack_s, pack_r, g_ss.at[0], g_rs.at[0], partner)
    g_cp.start()

    def quarter(k, off, width):
        return pl.ds(pl.multiple_of(((z + k) % 4) * QD + off, 512), width)

    d_cp = {}
    for u, (k, off, width) in enumerate(PIECES):

        @pl.loop(0, width // 512)
        def _(n):
            cs = pl.ds(pl.multiple_of(((z + k) % 4) * QD + off + n * 512, 512), 512)
            a = dot(smat[...], mixed_ref[:, cs])
            b = dot(smat[...], gtok_ref[:, cs]) * gcol[:, 0:1]
            send[:, :, cs] = join_rows(a, b)

        cols = quarter(k, off, width)
        for i in range(SLOTS):
            src, dst = send.at[i, :, cols], rx.at[i, :, cols]
            n = u * SLOTS + i
            if i == OWN:
                d_cp[u, i] = pltpu.make_async_copy(src, dst, loc.at[4 + u])
            else:
                d_cp[u, i] = remote(src, dst, d_ss.at[n], d_rs.at[n], to_expert(i))
            d_cp[u, i].start()

    fs[...] = jnp.zeros_like(fs)
    put(0, sel[0] * pack_s[2:3, :] + sel[1] * pack_s[3:4, :], sel[0] + sel[1])
    g_cp.wait()
    t0, t1, tsel = tables(pack_r[...], 1 - xh)
    put(1, tsel, t0 + t1)
    z_cp = []
    for u, (k, off, width) in enumerate(PIECES):
        for i in range(SLOTS):
            if i == OWN:
                d_cp[u, i].wait()
            else:
                d_cp[u, i].wait_recv()
        if k > 0:
            cp = remote(
                rx.at[:, :, quarter(k, off, width)], xdz.at[k - 1, :, :, pl.ds(off, width)],
                z_ss.at[u], z_rs.at[u], z_peer(k),
            )
            cp.start()
            z_cp.append(cp)
        if u == 0:
            ld_win.wait()
            ld_wout.wait()

        @pl.loop(0, width // 512)
        def _(n):
            ks = pl.ds(pl.multiple_of(((z + k) % 4) * QD + off + n * 512, 512), 512)
            xk, dk = split_rows(rx[:, :, ks])
            fs[0:ROWS, :] += dot(xk, win[ks, 0:F])
            fs[ROWS:2 * ROWS, :] += dot(xk, win[ks, F:2 * F])
            fs[2 * ROWS:3 * ROWS, :] += dot_nt(dk, wout[:, ks])

    @pl.loop(0, 8)
    def _(n):
        r = pl.multiple_of(n * 48, 48)
        g = fs[pl.ds(r, 48), :]
        u = fs[pl.ds(r + ROWS, 48), :]
        dh = fs[pl.ds(r + 2 * ROWS, 48), :]
        s = jax.nn.sigmoid(g)
        h = (g * s * u).astype(BF)
        rs = pl.ds(r, 48)
        agb[2, 3, rs, :] = h
        agb[0, 3, rs, :] = (dh * u * s * (1.0 + g * (1.0 - s))).astype(BF)
        agb[1, 3, rs, :] = (dh * g * s).astype(BF)
        sval[rs, :] = jnp.broadcast_to(jnp.sum(h.astype(F32) * dh, axis=1, keepdims=True), (48, TOK))

    a_cp = {}

    def gather_start(p):
        for k in (1, 3):
            n = p * 4 + k
            a_cp[p, k] = remote(agb.at[p, 3], agb.at[p, k - 1], a_ss.at[n], a_rs.at[n], z_peer(k))
            a_cp[p, k].start()

    def gather_pass(p):
        for k, cols in ((1, pl.ds(0, F // 2)), (3, pl.ds(F // 2, F // 2))):
            a_cp[p, k].wait_recv()
            n = p * 4 + k - 1
            a_cp[p, k - 1] = remote(
                agb.at[p, k - 1, :, cols], agb.at[p, 1, :, cols], a_ss.at[n], a_rs.at[n], z_peer(k)
            )
            a_cp[p, k - 1].start()

    def gather_end(p):
        a_cp[p, 0].wait_recv()
        a_cp[p, 2].wait_recv()

    gather_start(2)
    gather_start(0)

    for u in range(len(PIECES)):
        for i in range(SLOTS):
            if i != OWN:
                d_cp[u, i].wait_send()

    o_cp, s_cp = {}, {}

    def give(t, f):
        top = f * HALF
        for q in range(2):

            @pl.loop(0, 2)
            def _(n):
                parts = []
                for side in range(2):
                    cs = pl.ds(pl.multiple_of((2 * q + side) * QD + n * 512, 512), 512)
                    if t:
                        part = dot_nt(agb[0, 3, top:top + HALF, :], win[cs, 0:F])
                        part += dot_nt(agb[1, 3, top:top + HALF, :], win[cs, F:2 * F])
                    else:
                        part = dot(agb[2, 3, top:top + HALF, :], wout[:, cs])
                    parts.append(part)
                ws = pl.ds(pl.multiple_of(t * HD + q * QD + n * 512, 512), 512)
                send[8 * f:8 * f + 8, :, ws] = join_rows(*parts)

            for p in range(8):
                src = send.at[8 * f + p, :, pl.ds(t * HD + q * QD, QD)]
                dst = ro_hbm.at[pl.ds((2 * t + f) * ROWS + p * 48, 48), pl.ds(q * QD, QD)]
                n = ((t * 2 + f) * 2 + q) * 8 + p
                if p == OWN:
                    cp = pltpu.make_async_copy(src, dst, loc.at[11 + (t * 2 + f) * 2 + q])
                else:
                    cp = remote(src, dst, o_ss.at[n], o_rs.at[n], to_source(p))
                cp.start()
                o_cp[t, f, q, p] = cp

    give(0, 1)
    give(1, 1)
    for i in range(SLOTS):
        rows = pl.ds(i * CAP, CAP)
        if i == OWN:
            s_cp[i] = pltpu.make_async_copy(sval.at[rows], sret.at[rows], loc.at[10])
        else:
            s_cp[i] = remote(sval.at[rows], sret.at[rows], s_ss.at[i], s_rs.at[i], to_source(i))
        s_cp[i].start()
    give(0, 0)
    give(1, 0)

    p_cp = {}

    def relay(t, f, q):
        for p in range(8):
            if p == OWN:
                o_cp[t, f, q, p].wait()
            else:
                o_cp[t, f, q, p].wait_recv()
        cols = pl.ds(q * QD, QD)
        ld = pltpu.make_async_copy(
            ro_hbm.at[pl.ds((2 * t + f) * ROWS, ROWS), cols], wout.at[256:640, cols],
            loc.at[19 + (t * 2 + f) * 2 + q],
        )
        ld.start()
        ld.wait()
        if f == 0:
            p_cp[t, q].wait()
        own = gtok_ref if t else mixed_ref
        rows = pl.ds(f * TOK, TOK)

        @pl.loop(0, 2)
        def _(n):
            ws = pl.ds(pl.multiple_of(q * QD + n * 512, 512), 512)
            for side, block in enumerate(split_rows(wout[256:640, ws].reshape(8, 48, 512))):
                cs = pl.ds(pl.multiple_of((2 * q + side) * QD + n * 512, 512), 512)
                if t:
                    part = dot(stmat[rows, :], block)
                else:
                    part = dot(gmat[0, rows, :], block) + dot(gmat[1, rows, :], block)
                if f:
                    wout[TOK * t:TOK * (t + 1), cs] = part.astype(BF)
                else:
                    own[:, cs] = (part + pr[t, :, cs].astype(F32)).astype(BF)

        if f:
            n = 2 * t + q
            cs = pl.ds(q * HD, HD)
            p_cp[t, q] = remote(
                wout.at[TOK * t:TOK * (t + 1), cs], pr.at[t, :, cs], p_ss.at[n], p_rs.at[n], partner
            )
            p_cp[t, q].start()

    own0 = z * QD
    e_cp = {}
    GS = 512
    GT = 896

    DC = 1280
    XT = 2816

    def arrange():
        for cp in z_cp:
            cp.wait()
        for s in range(4):

            @pl.loop(0, 4)
            def _(n):
                n0 = pl.multiple_of(n * 256, 256)
                if s < 3:
                    blk = xdz[s, :, :, pl.ds(n0, 256)]
                else:
                    blk = rx[:, :, pl.ds(pl.multiple_of(own0 + n0, 256), 256)]
                xk, dk = split_rows(blk)
                win[DC + s * ROWS:DC + (s + 1) * ROWS, pl.ds(n0, 256)] = dk
                win[pl.ds(XT + n0, 256), s * ROWS:(s + 1) * ROWS] = xk.T

    def grad_out():
        gather_end(2)

        @pl.loop(0, 3)
        def _(n):
            n0 = pl.multiple_of(n * 256, 256)
            h = agb[2, :, :, pl.ds(n0, 256)].reshape(4 * ROWS, 256)
            go[pl.ds(n0, 256), :] = dot_tn(h, win[DC:DC + 4 * ROWS, 0:QD])

        for q in range(4):
            r = pl.multiple_of(q * 192 + (1 - xl) * 96, 96)
            win[GS + q * 96:GS + (q + 1) * 96, 0:QD] = go[pl.ds(r, 96), :].astype(BF)
        e_cp[2] = remote(win.at[GS:GS + 384, 0:QD], gr_out, e_ss.at[2], e_rs.at[2], pair)
        e_cp[2].start()

    def grad_in(p):
        gather_end(p)

        def half(side, store):
            @pl.loop(0, 2)
            def _(n):
                n0 = pl.multiple_of(n * 256, 256)
                r = pl.multiple_of(XT + side * 512 + n0, 256)
                store(n0, dot(win[pl.ds(r, 256), :], agb[p].reshape(4 * ROWS, F)))

        def store_send(n0, acc):
            win[pl.ds(n0, 256), p * F:(p + 1) * F] = acc.astype(BF)

        def store_own(n0, acc):
            fs[pl.ds(p * 512 + n0, 256), :] = acc

        half(1 - xl, store_send)
        e_cp[p] = remote(win.at[0:512, p * F:(p + 1) * F], gr_in.at[p], e_ss.at[p], e_rs.at[p], pair)
        e_cp[p].start()
        half(xl, store_own)

    t_cp = []

    def out_rows():
        e_cp[2].wait()
        for q in range(4):
            r = pl.multiple_of(q * 192 + xl * 96, 96)
            win[GT + q * 96:GT + (q + 1) * 96, 0:QD] = (
                go[pl.ds(r, 96), :] + gr_out[q * 96:(q + 1) * 96, :].astype(F32)
            ).astype(BF)
        for k in (1, 2, 3):
            r = pl.multiple_of(GT + ((z + k) % 4) * 96, 32)
            cp = remote(
                win.at[pl.ds(r, 96), 0:QD], gt_r.at[k - 1], t_ss.at[k - 1], t_rs.at[k - 1], z_peer(k)
            )
            cp.start()
            t_cp.append(cp)
        gout_ref[:, pl.ds(pl.multiple_of(own0, QD), QD)] = win[pl.ds(pl.multiple_of(GT + z * 96, 32), 96), 0:QD]

    relay(0, 1, 0)
    relay(0, 1, 1)
    gather_pass(2)
    gather_start(1)
    relay(1, 1, 0)
    relay(1, 1, 1)
    arrange()
    gather_pass(0)
    grad_out()
    relay(0, 0, 0)
    gather_pass(1)
    grad_in(0)
    grad_in(1)
    relay(0, 0, 1)
    out_rows()
    relay(1, 0, 0)
    relay(1, 0, 1)

    for i in range(SLOTS):
        s_cp[i].wait()
    for k in range(2):
        ggate_ref[k:k + 1, :] = (
            jnp.sum(sel[k] * sret[...], axis=0, keepdims=True) / gates_ref[k:k + 1, :]
        )
    out_cp = []

    def leave(src, dst):
        cp = pltpu.make_async_copy(src, dst, out_sem.at[len(out_cp)])
        cp.start()
        out_cp.append(cp)

    for k in (1, 2, 3):
        t_cp[k - 1].wait()
        col = pl.multiple_of(((z + 4 - k) % 4) * QD, QD)
        gout_ref[:, pl.ds(col, QD)] = gt_r[k - 1]
    leave(gout_ref, gout_out)
    leave(mixed_ref, mixed_out)
    leave(gtok_ref, gtok_out)
    for p in range(2):
        e_cp[p].wait()
        cs = pl.ds(p * F, F)
        gin_ref[:, cs] = (fs[p * 512:(p + 1) * 512, :] + gr_in[p].astype(F32)).astype(BF)
        leave(gin_ref.at[:, cs], gin_out.at[:, cs])

    for p in range(3):
        for k in range(4):
            a_cp[p, k].wait_send()
    for n, cp in o_cp.items():
        if n[3] != OWN:
            cp.wait_send()
    for cp in out_cp:
        cp.wait()


def hand_over(*refs):
    ins, outs, held, sems = refs[:5], refs[5:10], refs[10:15], refs[15]
    loads = [pltpu.make_async_copy(ins[n], held[n], sems.at[n]) for n in range(5)]
    stores = [pltpu.make_async_copy(held[n], outs[n], sems.at[5 + n]) for n in range(5)]
    for cp in loads:
        cp.start()
    for n in range(5):
        loads[n].wait()
        stores[n].start()
    for cp in stores:
        cp.wait()


def shards(tokens, gates, routes, w_in, w_out, cotangent):
    hbm = pl.BlockSpec(memory_space=pl.ANY)
    vm = pl.BlockSpec(memory_space=pltpu.VMEM)
    dma = pltpu.SemaphoreType.DMA
    outs = pl.pallas_call(
        kernel,
        name="experts",
        out_shape=(
            jax.ShapeDtypeStruct((TOK, D), BF),
            jax.ShapeDtypeStruct((TOK, D), BF),
            jax.ShapeDtypeStruct((2, TOK), F32),
            jax.ShapeDtypeStruct((512, 2 * F), BF),
            jax.ShapeDtypeStruct((96, D), BF),
            jax.ShapeDtypeStruct((4 * ROWS, HD), BF),
        ),
        in_specs=[hbm, hbm, vm, vm, hbm, hbm],
        out_specs=(hbm, hbm, vm, hbm, hbm, hbm),
        scratch_shapes=[
            pltpu.VMEM((TOK, D), BF),
            pltpu.VMEM((TOK, D), BF),
            pltpu.VMEM((512, 2 * F), BF),
            pltpu.VMEM((96, D), BF),
            pltpu.VMEM((SLOTS, 48, D), BF),
            pltpu.VMEM((SLOTS, 48, D), BF),
            pltpu.VMEM((3, SLOTS, 48, QD), BF),
            pltpu.VMEM((D, 2 * F), BF),
            pltpu.VMEM((F, D), BF),
            pltpu.VMEM((3 * ROWS, F), F32),
            pltpu.VMEM((3, 4, ROWS, F), BF),
            pltpu.VMEM((F, QD), F32),
            pltpu.VMEM((2, 512, F), BF),
            pltpu.VMEM((384, QD), BF),
            pltpu.VMEM((3, 96, QD), BF),
            pltpu.VMEM((2, TOK, D), BF),
            pltpu.VMEM((2, ROWS, TOK), F32),
            pltpu.VMEM((ROWS, TOK), BF),
            pltpu.VMEM((8, TOK), F32),
            pltpu.VMEM((8, TOK), F32),
            pltpu.VMEM((ROWS, TOK), F32),
            pltpu.VMEM((2 * TOK, ROWS // 2), BF),
            pltpu.VMEM((2, 2 * TOK, ROWS // 2), BF),
            pltpu.VMEM((ROWS, TOK), F32),
            pltpu.VMEM((ROWS, TOK), F32),
            dma((len(PIECES) * SLOTS,)), dma((len(PIECES) * SLOTS,)),
            dma((len(PIECES),)), dma((len(PIECES),)),
            dma((12,)), dma((12,)),
            dma((64,)), dma((64,)),
            dma((SLOTS,)), dma((SLOTS,)),
            dma((3,)), dma((3,)),
            dma((3,)), dma((3,)),
            dma((1,)), dma((1,)),
            dma((4,)), dma((4,)),
            dma((27,)),
            dma((5,)),
        ],
        compiler_params=pltpu.CompilerParams(
            collective_id=0, has_side_effects=True, vmem_limit_bytes=64 * 2**20 - 65536
        ),
    )(tokens, cotangent, routes.T, gates.T, w_in, w_out)
    outs = pl.pallas_call(
        hand_over,
        name="hand_over",
        out_shape=tuple(jax.ShapeDtypeStruct(o.shape, o.dtype) for o in outs[:5]),
        in_specs=[hbm] * 5,
        out_specs=(hbm,) * 5,
        scratch_shapes=[pltpu.VMEM(o.shape, o.dtype) for o in outs[:5]] + [dma((10,))],
    )(*outs[:5])
    return outs[0], outs[1], outs[2].T, outs[3], outs[4]


def solution(mesh):
    rows = P(("tensor", "context", "dp"), None)
    experts = P(("tensor", "context"), None, None)
    return jax.shard_map(
        shards,
        mesh=mesh,
        in_specs=(rows, rows, rows, experts, experts, rows),
        out_specs=(rows, rows, rows, rows, rows),
        check_vma=False,
    )
```

```python
import jax
import jax.numpy as jnp
from jax import lax
from jax.experimental import pallas as pl
from jax.experimental.pallas import tpu as pltpu
from jax.sharding import PartitionSpec as P

MESH = pl.DeviceIdType.MESH
BF = jnp.bfloat16
F32 = jnp.float32

D = 4096
F = 768
CAP = 24
SLOTS = 16
ROWS = SLOTS * CAP
TOK = 128
OWN = 6
PIECES = ((2, 0, 1024), (1, 0, 1024), (3, 0, 1024), (0, 0, 512), (0, 512, 512))
QD = D // 4
HD = D // 2


def dot(a, b):
    return jnp.dot(a, b, preferred_element_type=F32)


def dot_nt(a, b):
    return lax.dot_general(a, b, (((1,), (1,)), ((), ())), preferred_element_type=F32)


def dot_tn(a, b):
    return lax.dot_general(a, b, (((0,), (0,)), ((), ())), preferred_element_type=F32)


def split_rows(block):
    wide = block.astype(F32)
    rows, n = wide.shape[0] * CAP, wide.shape[-1]
    first = wide[:, :CAP, :].reshape(rows, n).astype(BF)
    last = wide[:, CAP:, :].reshape(rows, n).astype(BF)
    return first, last


def join_rows(first, last):
    n = first.shape[-1]
    s = first.shape[0] // CAP
    return jnp.concatenate([first.reshape(s, CAP, n), last.reshape(s, CAP, n)], axis=1).astype(BF)


def kernel(
    tok_hbm, cot_hbm, routes_ref, gates_ref, win_hbm, wout_hbm,
    mixed_out, gtok_out, ggate_ref, gin_out, gout_out, ro_hbm,
    mixed_ref, gtok_ref, gin_ref, gout_ref,
    send, rx, xdz, win, wout, fs, agb, go, gr_in, gr_out, gt_r, pr,
    sel, smat, pack_s, pack_r, gcol, stmat, gmat, sval, sret,
    d_ss, d_rs, z_ss, z_rs, a_ss, a_rs, o_ss, o_rs, s_ss, s_rs, e_ss, e_rs, t_ss, t_rs,
    g_ss, g_rs, p_ss, p_rs, loc, out_sem,
):
    y = lax.axis_index("tensor")
    c = lax.axis_index("context")
    d = lax.axis_index("dp")
    z = d // 2
    xl = d % 2
    xh = c // 2
    co = c % 2

    def context_of(i):
        return (1 - xh if i // 8 else xh) * 2 + (1 - co if i % 2 else co)

    def to_expert(i):
        return ((y + 1 + i % 8 // 2) % 4, context_of(i), d)

    def to_source(i):
        return ((y + 3 - i % 8 // 2) % 4, context_of(i), d)

    def z_peer(k):
        return (y, c, ((z + k) % 4) * 2 + xl)

    pair = (y, c, z * 2 + (1 - xl))
    partner = to_expert(OWN + 8)

    def remote(src, dst, ss, rs, dev):
        return pltpu.make_async_remote_copy(
            src_ref=src, dst_ref=dst, send_sem=ss, recv_sem=rs, device_id=dev, device_id_type=MESH
        )

    ld_tok = pltpu.make_async_copy(tok_hbm, mixed_ref, loc.at[0])
    ld_cot = pltpu.make_async_copy(cot_hbm, gtok_ref, loc.at[1])
    ld_win = pltpu.make_async_copy(win_hbm.at[0], win, loc.at[2])
    ld_wout = pltpu.make_async_copy(wout_hbm.at[0], wout, loc.at[3])
    ld_tok.start()
    ld_cot.start()

    bar = pltpu.get_barrier_semaphore()
    for i in range(SLOTS):
        if i != OWN:
            pl.semaphore_signal(bar, inc=1, device_id=to_expert(i), device_id_type=MESH)
    for k in (1, 2, 3):
        pl.semaphore_signal(bar, inc=1, device_id=z_peer(k), device_id_type=MESH)
    pl.semaphore_signal(bar, inc=1, device_id=pair, device_id_type=MESH)

    pack_s[0:2, :] = routes_ref[...].astype(F32)
    pack_s[2:4, :] = gates_ref[...]
    row = lax.broadcasted_iota(jnp.int32, (ROWS, TOK), 0)
    slot = (row * 683) >> 14
    place = (row - slot * CAP).astype(F32)
    far = slot >> 3
    ahead = ((y + 1 + ((slot >> 1) & 3)) & 3) * 4 + (co ^ (slot & 1))
    before = jnp.where(
        lax.broadcasted_iota(jnp.int32, (TOK, TOK), 0) < lax.broadcasted_iota(jnp.int32, (TOK, TOK), 1),
        1.0, 0.0,
    ).astype(BF)

    def tables(pack, half):
        r0, r1 = pack[0:1, :], pack[1:2, :]
        expert = (ahead + (half ^ far) * 2).astype(F32)
        ids = lax.broadcasted_iota(jnp.int32, (SLOTS, TOK), 0).astype(F32)
        match = jnp.where((ids == r0) | (ids == r1), 1.0, 0.0).astype(BF)
        rank = dot(match, before).astype(BF)
        pick = jnp.where(
            expert[:, :SLOTS] == lax.broadcasted_iota(jnp.int32, (ROWS, SLOTS), 1).astype(F32), 1.0, 0.0
        ).astype(BF)
        here = dot(pick, rank) == place
        s0 = jnp.where((expert == r0) & here, 1.0, 0.0)
        s1 = jnp.where((expert == r1) & here, 1.0, 0.0)
        return s0, s1, s0 * pack[2:3, :] + s1 * pack[3:4, :]

    s0, s1, gsel = tables(pack_s[...], xh)
    sel[0] = s0
    sel[1] = s1
    smat[...] = (s0 + s1).astype(BF)
    gcol[...] = jnp.broadcast_to(jnp.sum(gsel, axis=1, keepdims=True), (ROWS, TOK))

    HALF = ROWS // 2

    def put(half, gates, chosen):
        rows = pl.ds(half * TOK, TOK)
        cut = slice(half * HALF, (half + 1) * HALF)
        gt = gates.T
        ghi = gt.astype(BF)
        gmat[0, rows, :] = ghi[:, cut]
        gmat[1, rows, :] = (gt - ghi.astype(F32)).astype(BF)[:, cut]
        stmat[rows, :] = chosen.T.astype(BF)[:, cut]

    ld_tok.wait()
    ld_cot.wait()
    ld_win.start()
    ld_wout.start()
    pl.semaphore_wait(bar, 19)

    g_cp = remote(pack_s, pack_r, g_ss.at[0], g_rs.at[0], partner)
    g_cp.start()

    def quarter(k, off, width):
        return pl.ds(pl.multiple_of(((z + k) % 4) * QD + off, 512), width)

    d_cp = {}
    for u, (k, off, width) in enumerate(PIECES):

        @pl.loop(0, width // 512)
        def _(n):
            cs = pl.ds(pl.multiple_of(((z + k) % 4) * QD + off + n * 512, 512), 512)
            a = dot(smat[...], mixed_ref[:, cs])
            b = dot(smat[...], gtok_ref[:, cs]) * gcol[:, 0:1]
            send[:, :, cs] = join_rows(a, b)

        cols = quarter(k, off, width)
        for i in range(SLOTS):
            src, dst = send.at[i, :, cols], rx.at[i, :, cols]
            n = u * SLOTS + i
            if i == OWN:
                d_cp[u, i] = pltpu.make_async_copy(src, dst, loc.at[4 + u])
            else:
                d_cp[u, i] = remote(src, dst, d_ss.at[n], d_rs.at[n], to_expert(i))
            d_cp[u, i].start()

    fs[...] = jnp.zeros_like(fs)
    put(0, sel[0] * pack_s[2:3, :] + sel[1] * pack_s[3:4, :], sel[0] + sel[1])
    g_cp.wait()
    t0, t1, tsel = tables(pack_r[...], 1 - xh)
    put(1, tsel, t0 + t1)
    z_cp = []
    for u, (k, off, width) in enumerate(PIECES):
        for i in range(SLOTS):
            if i == OWN:
                d_cp[u, i].wait()
            else:
                d_cp[u, i].wait_recv()
        if k > 0:
            cp = remote(
                rx.at[:, :, quarter(k, off, width)], xdz.at[k - 1, :, :, pl.ds(off, width)],
                z_ss.at[u], z_rs.at[u], z_peer(k),
            )
            cp.start()
            z_cp.append(cp)
        if u == 0:
            ld_win.wait()
            ld_wout.wait()

        @pl.loop(0, width // 512)
        def _(n):
            ks = pl.ds(pl.multiple_of(((z + k) % 4) * QD + off + n * 512, 512), 512)
            xk, dk = split_rows(rx[:, :, ks])
            fs[0:ROWS, :] += dot(xk, win[ks, 0:F])
            fs[ROWS:2 * ROWS, :] += dot(xk, win[ks, F:2 * F])
            fs[2 * ROWS:3 * ROWS, :] += dot_nt(dk, wout[:, ks])

    @pl.loop(0, 8)
    def _(n):
        r = pl.multiple_of(n * 48, 48)
        g = fs[pl.ds(r, 48), :]
        u = fs[pl.ds(r + ROWS, 48), :]
        dh = fs[pl.ds(r + 2 * ROWS, 48), :]
        s = jax.nn.sigmoid(g)
        h = (g * s * u).astype(BF)
        rs = pl.ds(r, 48)
        agb[2, 3, rs, :] = h
        agb[0, 3, rs, :] = (dh * u * s * (1.0 + g * (1.0 - s))).astype(BF)
        agb[1, 3, rs, :] = (dh * g * s).astype(BF)
        sval[rs, :] = jnp.broadcast_to(jnp.sum(h.astype(F32) * dh, axis=1, keepdims=True), (48, TOK))

    a_cp = {}

    def gather_start(p):
        for k in (1, 3):
            n = p * 4 + k
            a_cp[p, k] = remote(agb.at[p, 3], agb.at[p, k - 1], a_ss.at[n], a_rs.at[n], z_peer(k))
            a_cp[p, k].start()

    def gather_pass(p):
        for k, cols in ((1, pl.ds(0, F // 2)), (3, pl.ds(F // 2, F // 2))):
            a_cp[p, k].wait_recv()
            n = p * 4 + k - 1
            a_cp[p, k - 1] = remote(
                agb.at[p, k - 1, :, cols], agb.at[p, 1, :, cols], a_ss.at[n], a_rs.at[n], z_peer(k)
            )
            a_cp[p, k - 1].start()

    def gather_end(p):
        a_cp[p, 0].wait_recv()
        a_cp[p, 2].wait_recv()

    gather_start(2)
    gather_start(0)

    for u in range(len(PIECES)):
        for i in range(SLOTS):
            if i != OWN:
                d_cp[u, i].wait_send()

    o_cp, s_cp = {}, {}

    def give(t, f):
        top = f * HALF
        for q in range(2):

            @pl.loop(0, 2)
            def _(n):
                parts = []
                for side in range(2):
                    cs = pl.ds(pl.multiple_of((2 * q + side) * QD + n * 512, 512), 512)
                    if t:
                        part = dot_nt(agb[0, 3, top:top + HALF, :], win[cs, 0:F])
                        part += dot_nt(agb[1, 3, top:top + HALF, :], win[cs, F:2 * F])
                    else:
                        part = dot(agb[2, 3, top:top + HALF, :], wout[:, cs])
                    parts.append(part)
                ws = pl.ds(pl.multiple_of(t * HD + q * QD + n * 512, 512), 512)
                send[8 * f:8 * f + 8, :, ws] = join_rows(*parts)

            for p in range(8):
                src = send.at[8 * f + p, :, pl.ds(t * HD + q * QD, QD)]
                dst = ro_hbm.at[pl.ds((2 * t + f) * ROWS + p * 48, 48), pl.ds(q * QD, QD)]
                n = ((t * 2 + f) * 2 + q) * 8 + p
                if p == OWN:
                    cp = pltpu.make_async_copy(src, dst, loc.at[11 + (t * 2 + f) * 2 + q])
                else:
                    cp = remote(src, dst, o_ss.at[n], o_rs.at[n], to_source(p))
                cp.start()
                o_cp[t, f, q, p] = cp

    give(0, 1)
    give(1, 1)
    for i in range(SLOTS):
        rows = pl.ds(i * CAP, CAP)
        if i == OWN:
            s_cp[i] = pltpu.make_async_copy(sval.at[rows], sret.at[rows], loc.at[10])
        else:
            s_cp[i] = remote(sval.at[rows], sret.at[rows], s_ss.at[i], s_rs.at[i], to_source(i))
        s_cp[i].start()
    give(0, 0)
    give(1, 0)

    p_cp = {}

    def relay(t, f, q):
        for p in range(8):
            if p == OWN:
                o_cp[t, f, q, p].wait()
            else:
                o_cp[t, f, q, p].wait_recv()
        cols = pl.ds(q * QD, QD)
        ld = pltpu.make_async_copy(
            ro_hbm.at[pl.ds((2 * t + f) * ROWS, ROWS), cols], wout.at[256:640, cols],
            loc.at[19 + (t * 2 + f) * 2 + q],
        )
        ld.start()
        ld.wait()
        if f == 0:
            p_cp[t, q].wait()
        own = gtok_ref if t else mixed_ref
        rows = pl.ds(f * TOK, TOK)

        @pl.loop(0, 2)
        def _(n):
            ws = pl.ds(pl.multiple_of(q * QD + n * 512, 512), 512)
            for side, block in enumerate(split_rows(wout[256:640, ws].reshape(8, 48, 512))):
                cs = pl.ds(pl.multiple_of((2 * q + side) * QD + n * 512, 512), 512)
                if t:
                    part = dot(stmat[rows, :], block)
                else:
                    part = dot(gmat[0, rows, :], block) + dot(gmat[1, rows, :], block)
                if f:
                    wout[TOK * t:TOK * (t + 1), cs] = part.astype(BF)
                else:
                    own[:, cs] = (part + pr[t, :, cs].astype(F32)).astype(BF)

        if f:
            n = 2 * t + q
            cs = pl.ds(q * HD, HD)
            p_cp[t, q] = remote(
                wout.at[TOK * t:TOK * (t + 1), cs], pr.at[t, :, cs], p_ss.at[n], p_rs.at[n], partner
            )
            p_cp[t, q].start()

    own0 = z * QD
    e_cp = {}
    GS = 512
    GT = 896

    DC = 1280
    XT = 2816

    def arrange():
        for cp in z_cp:
            cp.wait()
        for s in range(4):

            @pl.loop(0, 4)
            def _(n):
                n0 = pl.multiple_of(n * 256, 256)
                if s < 3:
                    blk = xdz[s, :, :, pl.ds(n0, 256)]
                else:
                    blk = rx[:, :, pl.ds(pl.multiple_of(own0 + n0, 256), 256)]
                xk, dk = split_rows(blk)
                win[DC + s * ROWS:DC + (s + 1) * ROWS, pl.ds(n0, 256)] = dk
                win[pl.ds(XT + n0, 256), s * ROWS:(s + 1) * ROWS] = xk.T

    def grad_out():
        gather_end(2)

        @pl.loop(0, 3)
        def _(n):
            n0 = pl.multiple_of(n * 256, 256)
            h = agb[2, :, :, pl.ds(n0, 256)].reshape(4 * ROWS, 256)
            go[pl.ds(n0, 256), :] = dot_tn(h, win[DC:DC + 4 * ROWS, 0:QD])

        for q in range(4):
            r = pl.multiple_of(q * 192 + (1 - xl) * 96, 96)
            win[GS + q * 96:GS + (q + 1) * 96, 0:QD] = go[pl.ds(r, 96), :].astype(BF)
        e_cp[2] = remote(win.at[GS:GS + 384, 0:QD], gr_out, e_ss.at[2], e_rs.at[2], pair)
        e_cp[2].start()

    def grad_in(p):
        gather_end(p)

        def half(side, store):
            @pl.loop(0, 2)
            def _(n):
                n0 = pl.multiple_of(n * 256, 256)
                r = pl.multiple_of(XT + side * 512 + n0, 256)
                store(n0, dot(win[pl.ds(r, 256), :], agb[p].reshape(4 * ROWS, F)))

        def store_send(n0, acc):
            win[pl.ds(n0, 256), p * F:(p + 1) * F] = acc.astype(BF)

        def store_own(n0, acc):
            fs[pl.ds(p * 512 + n0, 256), :] = acc

        half(1 - xl, store_send)
        e_cp[p] = remote(win.at[0:512, p * F:(p + 1) * F], gr_in.at[p], e_ss.at[p], e_rs.at[p], pair)
        e_cp[p].start()
        half(xl, store_own)

    t_cp = []

    def out_rows():
        e_cp[2].wait()
        for q in range(4):
            r = pl.multiple_of(q * 192 + xl * 96, 96)
            win[GT + q * 96:GT + (q + 1) * 96, 0:QD] = (
                go[pl.ds(r, 96), :] + gr_out[q * 96:(q + 1) * 96, :].astype(F32)
            ).astype(BF)
        for k in (1, 2, 3):
            r = pl.multiple_of(GT + ((z + k) % 4) * 96, 32)
            cp = remote(
                win.at[pl.ds(r, 96), 0:QD], gt_r.at[k - 1], t_ss.at[k - 1], t_rs.at[k - 1], z_peer(k)
            )
            cp.start()
            t_cp.append(cp)
        gout_ref[:, pl.ds(pl.multiple_of(own0, QD), QD)] = win[pl.ds(pl.multiple_of(GT + z * 96, 32), 96), 0:QD]

    relay(0, 1, 0)
    relay(0, 1, 1)
    gather_pass(2)
    gather_start(1)
    relay(1, 1, 0)
    relay(1, 1, 1)
    arrange()
    gather_pass(0)
    grad_out()
    relay(0, 0, 0)
    gather_pass(1)
    grad_in(0)
    grad_in(1)
    relay(0, 0, 1)
    out_rows()
    relay(1, 0, 0)
    relay(1, 0, 1)

    for i in range(SLOTS):
        s_cp[i].wait()
    for k in range(2):
        ggate_ref[k:k + 1, :] = (
            jnp.sum(sel[k] * sret[...], axis=0, keepdims=True) / gates_ref[k:k + 1, :]
        )
    out_cp = []

    def leave(src, dst):
        cp = pltpu.make_async_copy(src, dst, out_sem.at[len(out_cp)])
        cp.start()
        out_cp.append(cp)

    for k in (1, 2, 3):
        t_cp[k - 1].wait()
        col = pl.multiple_of(((z + 4 - k) % 4) * QD, QD)
        gout_ref[:, pl.ds(col, QD)] = gt_r[k - 1]
    leave(gout_ref, gout_out)
    leave(mixed_ref, mixed_out)
    leave(gtok_ref, gtok_out)
    for p in range(2):
        e_cp[p].wait()
        cs = pl.ds(p * F, F)
        gin_ref[:, cs] = (fs[p * 512:(p + 1) * 512, :] + gr_in[p].astype(F32)).astype(BF)
        leave(gin_ref.at[:, cs], gin_out.at[:, cs])

    for p in range(3):
        for k in range(4):
            a_cp[p, k].wait_send()
    for n, cp in o_cp.items():
        if n[3] != OWN:
            cp.wait_send()
    for cp in out_cp:
        cp.wait()


def hand_over(*refs):
    ins, outs, held, sems = refs[:5], refs[5:10], refs[10:15], refs[15]
    loads = [pltpu.make_async_copy(ins[n], held[n], sems.at[n]) for n in range(5)]
    stores = [pltpu.make_async_copy(held[n], outs[n], sems.at[5 + n]) for n in range(5)]
    for cp in loads:
        cp.start()
    for n in range(5):
        loads[n].wait()
        stores[n].start()
    for cp in stores:
        cp.wait()


def shards(tokens, gates, routes, w_in, w_out, cotangent):
    hbm = pl.BlockSpec(memory_space=pl.ANY)
    vm = pl.BlockSpec(memory_space=pltpu.VMEM)
    dma = pltpu.SemaphoreType.DMA
    outs = pl.pallas_call(
        kernel,
        name="experts",
        out_shape=(
            jax.ShapeDtypeStruct((TOK, D), BF),
            jax.ShapeDtypeStruct((TOK, D), BF),
            jax.ShapeDtypeStruct((2, TOK), F32),
            jax.ShapeDtypeStruct((512, 2 * F), BF),
            jax.ShapeDtypeStruct((96, D), BF),
            jax.ShapeDtypeStruct((4 * ROWS, HD), BF),
        ),
        in_specs=[hbm, hbm, vm, vm, hbm, hbm],
        out_specs=(hbm, hbm, vm, hbm, hbm, hbm),
        scratch_shapes=[
            pltpu.VMEM((TOK, D), BF),
            pltpu.VMEM((TOK, D), BF),
            pltpu.VMEM((512, 2 * F), BF),
            pltpu.VMEM((96, D), BF),
            pltpu.VMEM((SLOTS, 48, D), BF),
            pltpu.VMEM((SLOTS, 48, D), BF),
            pltpu.VMEM((3, SLOTS, 48, QD), BF),
            pltpu.VMEM((D, 2 * F), BF),
            pltpu.VMEM((F, D), BF),
            pltpu.VMEM((3 * ROWS, F), F32),
            pltpu.VMEM((3, 4, ROWS, F), BF),
            pltpu.VMEM((F, QD), F32),
            pltpu.VMEM((2, 512, F), BF),
            pltpu.VMEM((384, QD), BF),
            pltpu.VMEM((3, 96, QD), BF),
            pltpu.VMEM((2, TOK, D), BF),
            pltpu.VMEM((2, ROWS, TOK), F32),
            pltpu.VMEM((ROWS, TOK), BF),
            pltpu.VMEM((8, TOK), F32),
            pltpu.VMEM((8, TOK), F32),
            pltpu.VMEM((ROWS, TOK), F32),
            pltpu.VMEM((2 * TOK, ROWS // 2), BF),
            pltpu.VMEM((2, 2 * TOK, ROWS // 2), BF),
            pltpu.VMEM((ROWS, TOK), F32),
            pltpu.VMEM((ROWS, TOK), F32),
            dma((len(PIECES) * SLOTS,)), dma((len(PIECES) * SLOTS,)),
            dma((len(PIECES),)), dma((len(PIECES),)),
            dma((12,)), dma((12,)),
            dma((64,)), dma((64,)),
            dma((SLOTS,)), dma((SLOTS,)),
            dma((3,)), dma((3,)),
            dma((3,)), dma((3,)),
            dma((1,)), dma((1,)),
            dma((4,)), dma((4,)),
            dma((27,)),
            dma((5,)),
        ],
        compiler_params=pltpu.CompilerParams(
            collective_id=0, has_side_effects=True, vmem_limit_bytes=64 * 2**20 - 65536
        ),
    )(tokens, cotangent, routes.T, gates.T, w_in, w_out)
    outs = pl.pallas_call(
        hand_over,
        name="hand_over",
        out_shape=tuple(jax.ShapeDtypeStruct(o.shape, o.dtype) for o in outs[:5]),
        in_specs=[hbm] * 5,
        out_specs=(hbm,) * 5,
        scratch_shapes=[pltpu.VMEM(o.shape, o.dtype) for o in outs[:5]] + [dma((10,))],
    )(*outs[:5])
    return outs[0], outs[1], outs[2].T, outs[3], outs[4]


def solution(mesh):
    rows = P(("tensor", "context", "dp"), None)
    experts = P(("tensor", "context"), None, None)
    return jax.shard_map(
        shards,
        mesh=mesh,
        in_specs=(rows, rows, rows, experts, experts, rows),
        out_specs=(rows, rows, rows, rows, rows),
        check_vma=False,
    )
```
